32 devices in a mesh: grp: 4 (over y, x), band: 8 (over z, core).
Axes of the slice: x: 2, y: 2, z: 4, core: 2. Of those that a mesh axis runs over, the one named last changes fastest.
Arguments:
- frames: bfloat16 [4, 5, 16, 2048], P('grp', None, 'band'), may hold values from -6 to 6
- grid_size: int32 [4, 2], P('grp'), may hold values from 1 to 128, as said below
- out_grad: bfloat16 [4, 15, 16, 16384], P('grp', None, 'band'), may hold values from -6 to 6
- enc_hidden: float32 [512, 1152], P('band'), may hold values from -0.3125 to 0.3125
- enc_hidden_m: float32 [512, 1152], P('band'), may hold values from -32 to 32
- enc_hidden_v: float32 [512, 1152], P('band'), may hold values from 18.432 to 9437.184
- fore_hidden: float32 [512, 1152], P('band'), may hold values from -0.3125 to 0.3125
- fore_hidden_m: float32 [512, 1152], P('band'), may hold values from -224 to 224
- fore_hidden_v: float32 [512, 1152], P('band'), may hold values from 614.4 to 9830.4
- enc_input: float32 [512, 144], P('band'), may hold values from -0.5 to 0.5
- enc_input_m: float32 [512, 144], P('band'), may hold values from -128 to 128
- enc_input_v: float32 [512, 144], P('band'), may hold values from 204.8 to 104857.6
- cell_vectors: float32 [1792], P('band'), as said below
- vectors_m: float32 [1792], P('band'), may hold values from -640 to 640
- vectors_v: float32 [1792], P('band'), may hold values from 5529.6 to 88473.6
Outputs:
- h_out: bfloat16 [4, 15, 16, 16384], P('grp', None, 'band')
- d_frames: float32 [4, 5, 16, 2048], P('grp', None, 'band')
- enc_hidden_new: float32 [512, 1152], P('band')
- enc_hidden_m_new: float32 [512, 1152], P('band')
- enc_hidden_v_new: float32 [512, 1152], P('band')
- enc_hidden_bf16: bfloat16 [512, 1152], P('band')
- fore_hidden_new: float32 [512, 1152], P('band')
- fore_hidden_m_new: float32 [512, 1152], P('band')
- fore_hidden_v_new: float32 [512, 1152], P('band')
- fore_hidden_bf16: bfloat16 [512, 1152], P('band')
- enc_input_new: float32 [512, 144], P('band')
- enc_input_m_new: float32 [512, 144], P('band')
- enc_input_v_new: float32 [512, 144], P('band')
- enc_input_bf16: bfloat16 [512, 144], P('band')
- vectors_new: float32 [1792], P('band')
- vectors_m_new: float32 [1792], P('band')
- vectors_v_new: float32 [1792], P('band')
- vectors_bf16: bfloat16 [1792], P('band')
The draws below stay inside these ranges and needn't reach their ends.
Inputs may be any that keep to these rules, and one draw needn't show every extreme that they name: `grid_size`: row limit then column limit of each grid; 2 grids, drawn from the seed, have all 16 rows and 128 columns, the others between five and seven eighths of each. `cell_vectors`: for each of the two cells in turn: 128 biases for each of the gates i, f, g, o, then 128 peephole weights for each of i, f, o.
All inputs are finite; a program needn't handle non-finite values.
Results may differ from the reference program's by a relative error of at most 0.023.
Values may be sent and summed in bfloat16 or wider, within the bound.
No kernel may reach another device: no remote copies, remote signals or barrier semaphores. Data moves between devices by JAX's collectives and lax.ppermute only.
A program may use at most 64 MiB of HBM per device.

```python
import math
import jax
import jax.numpy as jnp
from jax import lax

HID = 128
CIN = 16
GATES = 512
COLS = 128
FRAMES_IN = 5
FRAMES_OUT = 15
STEP = 5
GRID_H = 16
N_GRP = 4


def draw_grid_size(key, part):
    key = jax.random.fold_in(key, 11)
    rank_key, row_key, col_key = jax.random.split(key, 3)
    rank_order = jax.random.permutation(rank_key, N_GRP)
    narrow_grid = rank_order >= N_GRP // 2
    row_small = jax.random.randint(row_key, (N_GRP,), GRID_H * 5 // 8, GRID_H * 7 // 8 + 1)
    col_small = jax.random.randint(col_key, (N_GRP,), COLS * 5 // 8, COLS * 7 // 8 + 1)
    row_total = jnp.where(narrow_grid, row_small, GRID_H)
    col_total = jnp.where(narrow_grid, col_small, COLS)
    return jnp.stack([row_total, col_total], axis=1).astype(jnp.int32)


def draw_cell_vectors(key, part):
    key = jax.random.fold_in(key, 12)
    key_list = jax.random.split(key, 3)
    biases = 0.3 * jax.random.normal(key_list[0], (2, 4, HID), jnp.float32)
    forget = jax.random.uniform(key_list[1], (2, 1, HID), jnp.float32, 1.0, 4.0)
    peeps = jax.random.uniform(key_list[2], (2, 3, HID), jnp.float32, -0.5, 0.5)
    gate_bias = jnp.concatenate([biases[:, :1], forget, biases[:, 2:]], axis=1)
    return jnp.concatenate([gate_bias, peeps], axis=1).reshape(14 * HID).astype(jnp.float32)


def spread_draw(key, shape, lowest, ratio):
    unit = jax.random.uniform(key, shape, jnp.float32, 0.0, 1.0)
    return (lowest * jnp.exp(unit * math.log(ratio))).astype(jnp.float32)


def draw_enc_hidden_v(key, part):
    key = jax.random.fold_in(key, 13)
    lowest = 0.00045 * N_GRP * GRID_H * COLS * FRAMES_IN
    return spread_draw(key, (4 * HID, 9 * HID), lowest, 16.0)


def draw_enc_input_v(key, part):
    key = jax.random.fold_in(key, 14)
    lowest = 0.005 * N_GRP * GRID_H * COLS * FRAMES_IN
    return spread_draw(key, (4 * HID, 9 * CIN), lowest, 16.0)


def block_levels(stream_key, shape, cuts, least, high):
    loudness = 1.0
    for dim, shards_of in cuts:
        heights = jax.random.uniform(jax.random.fold_in(jax.random.fold_in(stream_key, 6), dim), (shards_of,), jnp.float32, least / len(cuts), high / len(cuts))
        loudness = loudness * jnp.repeat(jnp.exp(heights), shape[dim] // shards_of).reshape((-1,) + (1,) * (len(shape) - 1 - dim))
    return loudness


def centred(own_key, dims, scale, bound, shards=(), held_as=jnp.bfloat16):
    entries = jax.random.normal(own_key, dims, jnp.float32) * scale
    if len(shards) > 0:
        entries = block_levels(own_key, dims, shards, -0.22, 0.18) * entries
    return jnp.clip(entries, min=-bound, max=bound).astype(held_as)


def setup_inputs(seed: int = 0) -> dict:
    key_of = jax.random.split(jax.random.key(seed), 16)
    return {
        "frames": centred(key_of[0], (N_GRP, FRAMES_IN, GRID_H, COLS * CIN), 1.0, 6.0, ((0, 4), (2, 8))),
        "grid_size": draw_grid_size(jax.random.fold_in(key_of[15], 71), 0),
        "out_grad": centred(key_of[2], (N_GRP, FRAMES_OUT, GRID_H, COLS * HID), 1.0, 6.0, ((0, 4), (2, 8))),
        "enc_hidden": centred(key_of[3], (GATES, 9 * HID), (3 * HID) ** -0.5, 0.3125, ((0, 8),), jnp.float32),
        "enc_hidden_m": centred(key_of[4], (GATES, 9 * HID), (0.03 * (N_GRP * GRID_H * COLS * FRAMES_IN) ** 0.5), 32.0, ((0, 8),), jnp.float32),
        "enc_hidden_v": draw_enc_hidden_v(jax.random.fold_in(key_of[15], 71), 0),
        "fore_hidden": centred(key_of[6], (GATES, 9 * HID), (3 * HID) ** -0.5, 0.3125, ((0, 8),), jnp.float32),
        "fore_hidden_m": centred(key_of[7], (GATES, 9 * HID), (0.1 * (N_GRP * GRID_H * COLS * FRAMES_OUT) ** 0.5), 224.0, ((0, 8),), jnp.float32),
        "fore_hidden_v": jnp.clip(jnp.exp(math.log(9830.4) - 2.7725887 * jax.random.uniform(key_of[8], (GATES, 9 * HID), jnp.float32) ** block_levels(key_of[8], (GATES, 9 * HID), ((0, 8),), -0.2, 0.2)), 614.4, 9830.4),
        "enc_input": centred(key_of[9], (GATES, 9 * CIN), (9 * CIN) ** -0.5, 0.5, ((0, 8),), jnp.float32),
        "enc_input_m": centred(key_of[10], (GATES, 9 * CIN), (0.1 * (N_GRP * GRID_H * COLS * FRAMES_IN) ** 0.5), 128.0, ((0, 8),), jnp.float32),
        "enc_input_v": draw_enc_input_v(jax.random.fold_in(key_of[15], 71), 0),
        "cell_vectors": draw_cell_vectors(jax.random.fold_in(key_of[15], 71), 0),
        "vectors_m": centred(key_of[13], (14 * HID,), (0.3 * (N_GRP * GRID_H * COLS * FRAMES_OUT) ** 0.5), 640.0, ((0, 8),), jnp.float32),
        "vectors_v": jnp.clip(jnp.exp(math.log(88473.6) - 2.7725887 * jax.random.uniform(key_of[14], (14 * HID,), jnp.float32) ** block_levels(key_of[14], (14 * HID,), ((0, 8),), -0.2, 0.2)), 5529.6, 88473.6),
    }


@jax.custom_vjp
def low(v):
    return lax.optimization_barrier(v.astype(jnp.bfloat16)).astype(jnp.float32)

@jax.custom_vjp
def low_back(v):
    return v

def low_keep(v):
    return (low(v), None)

def low_pass(kept, grad):
    return (grad,)

def back_keep(v):
    return (v, None)

def back_low(kept, grad):
    return (low(grad),)
low.defvjp(low_keep, low_pass)
low_back.defvjp(back_keep, back_low)
beta_first = 0.5
beta_second = 0.5
adam_epsilon = 1e-08
weight_decay = 0.01
matrix_rate = 0.03
vector_rate = 0.3

def cell_math(conv, state_prev, vector, cell_mask):
    width = state_prev.shape[-1]
    pre_act = conv + vector[:4 * width]
    gate_in = jax.nn.sigmoid(pre_act[..., :width] + vector[4 * width:5 * width] * state_prev)
    gate_keep = jax.nn.sigmoid(pre_act[..., width:2 * width] + vector[5 * width:6 * width] * state_prev)
    candidate = jnp.tanh(pre_act[..., 2 * width:3 * width])
    state_new = (gate_keep * state_prev + gate_in * candidate) * cell_mask
    gate_out = jax.nn.sigmoid(pre_act[..., 3 * width:] + vector[6 * width:] * state_new)
    return (gate_out * jnp.tanh(state_new), state_new)

def tap_product(field, weight):
    padded = jnp.pad(field, ((0, 0), (1, 1), (1, 1), (0, 0)))
    height = field.shape[1]
    breadth = field.shape[2]
    taps_weight = weight.reshape(weight.shape[0], 9, -1)
    total = jnp.zeros(field.shape[:3] + (weight.shape[0],), jnp.float32)
    for tap in range(9):
        piece = padded[:, tap // 3:tap // 3 + height, tap % 3:tap % 3 + breadth]
        total = total + jnp.einsum('nrwc,gc->nrwg', piece, taps_weight[:, tap], precision=lax.Precision.HIGHEST)
    return total

def adam_update(weight, moment_one, moment_two, grad, rate):
    first_new = beta_first * moment_one + (1.0 - beta_first) * grad
    second_new = beta_second * moment_two + (1.0 - beta_second) * grad * grad
    scale_one = 1.0 - beta_first ** STEP
    scale_two = 1.0 - beta_second ** STEP
    direction = first_new / scale_one / (jnp.sqrt(second_new / scale_two) + adam_epsilon)
    fresh = weight - rate * (direction + weight_decay * weight)
    return (fresh, first_new, second_new, fresh.astype(jnp.bfloat16))

def reference(frames, grid_size, out_grad, enc_hidden, enc_hidden_m, enc_hidden_v, fore_hidden, fore_hidden_m, fore_hidden_v, enc_input, enc_input_m, enc_input_v, cell_vectors, vectors_m, vectors_v):
    row_ids = lax.iota(jnp.int32, GRID_H)
    col_ids = lax.iota(jnp.int32, COLS)
    inside = (row_ids[None, :, None] < grid_size[:, 0][:, None, None]) & (col_ids[None, None, :] < grid_size[:, 1][:, None, None])
    cell_mask = inside.astype(jnp.float32)[..., None]

    def forward(enc_raw, fore_raw, input_raw, vector_raw, frames_wide):
        w_enc = low(enc_raw)
        w_fore = low(fore_raw)
        w_input = low(input_raw)
        vectors = low(vector_raw).reshape(2, 7 * HID)
        inputs = frames_wide.reshape(N_GRP, FRAMES_IN, GRID_H, COLS, CIN) * cell_mask[:, None]

        def enc_step(carry, input_frame):
            hidden, state = carry
            conv = low_back(tap_product(hidden, w_enc) + tap_product(input_frame, w_input))
            new_hidden, new_state = cell_math(conv, state, vectors[0], cell_mask)
            return ((low(new_hidden), new_state), None)
        zero_field = jnp.zeros((N_GRP, GRID_H, COLS, HID), jnp.float32)
        (hidden, state), _ = lax.scan(jax.checkpoint(enc_step), (zero_field, zero_field), jnp.moveaxis(inputs, 1, 0))

        def fore_step(carry, unused):
            hidden, state = carry
            conv = low_back(tap_product(hidden, w_fore))
            new_hidden, new_state = cell_math(conv, state, vectors[1], cell_mask)
            rounded = low(new_hidden)
            return ((rounded, new_state), rounded)
        _, outputs = lax.scan(jax.checkpoint(fore_step), (hidden, state), None, length=FRAMES_OUT)
        return jnp.moveaxis(outputs, 0, 1).reshape(N_GRP, FRAMES_OUT, GRID_H, COLS * HID)
    frames_wide = frames.astype(jnp.float32)
    result, pull = jax.vjp(forward, enc_hidden, fore_hidden, enc_input, cell_vectors, frames_wide)
    grad_enc, grad_fore, grad_input, grad_vector, grad_frames = pull(out_grad.astype(jnp.float32))
    enc_new, enc_one, enc_two, enc_copy = adam_update(enc_hidden, enc_hidden_m, enc_hidden_v, grad_enc, matrix_rate)
    fore_new, fore_one, fore_two, fore_copy = adam_update(fore_hidden, fore_hidden_m, fore_hidden_v, grad_fore, matrix_rate)
    input_new, input_one, input_two, input_copy = adam_update(enc_input, enc_input_m, enc_input_v, grad_input, matrix_rate)
    vector_new, vector_one, vector_two, vector_copy = adam_update(cell_vectors, vectors_m, vectors_v, grad_vector, vector_rate)
    return (result.astype(jnp.bfloat16), grad_frames, enc_new, enc_one, enc_two, enc_copy, fore_new, fore_one, fore_two, fore_copy, input_new, input_one, input_two, input_copy, vector_new, vector_one, vector_two, vector_copy)
```

```python
import functools

import jax
import jax.numpy as jnp
import numpy as np
from jax import lax
from jax.experimental import pallas as pl
from jax.experimental.pallas import tpu as pltpu
from jax.sharding import Mesh
from jax.sharding import PartitionSpec as P

HID = 128
FRAMES_IN = 5
FRAMES_OUT = 15
STEP = 5


beta_first = 0.5
beta_second = 0.5
adam_epsilon = 1e-08
weight_decay = 0.01
matrix_rate = 0.03
vector_rate = 0.3


def from_behind(value, axis, steps):
    count = lax.axis_size(axis)
    first, last = (max(0, -steps), min(count, count - steps))
    return lax.ppermute(value, axis, [(source, source + steps) for source in range(first, last)])


def cut_along(array, dim, peers):
    shape = array.shape
    tiles = array.reshape(*shape[:dim], peers, shape[dim] // peers, *shape[dim + 1 :])
    return jnp.moveaxis(tiles, dim, 0)


def summed_on_arrival(array, axis, dim):
    peers = lax.axis_size(axis)
    tiles = lax.all_to_all(cut_along(array, dim, peers), axis, 0, 0, tiled=True)
    return jnp.sum(tiles.astype(jnp.float32), axis=0)


def sent_together(arrays, axis, dim, along):
    widths = [a.shape[along] for a in arrays]
    both = jnp.concatenate(arrays, axis=along)
    result = summed_on_arrival(both, axis, dim)
    return tuple(jnp.split(result, [sum(widths[:k]) for k in range(1, len(widths))], axis=along))


def cell_math(conv, state_prev, vector, cell_mask):
    width = state_prev.shape[-1]
    pre_act = conv + vector[: 4 * width]
    gate_in = jax.nn.sigmoid(pre_act[..., :width] + vector[4 * width : 5 * width] * state_prev)
    gate_keep = jax.nn.sigmoid(
        pre_act[..., width : 2 * width] + vector[5 * width : 6 * width] * state_prev
    )
    candidate = jnp.tanh(pre_act[..., 2 * width : 3 * width])
    state_new = (gate_keep * state_prev + gate_in * candidate) * cell_mask
    gate_out = jax.nn.sigmoid(pre_act[..., 3 * width :] + vector[6 * width :] * state_new)
    return (gate_out * jnp.tanh(state_new), state_new)


def pad_columns(field):
    return jnp.pad(field, ((0, 0), (1, 1), (0, 0)))


def forward_taps(padded, row_count, col_count):
    pieces = [
        padded[tap_row : tap_row + row_count, tap_col : tap_col + col_count]
        for tap_row in range(3)
        for tap_col in range(3)
    ]
    return jnp.concatenate(pieces, axis=-1).reshape(row_count * col_count, -1)


def backward_taps(padded, row_count, col_count):
    pieces = [
        padded[2 - tap_row : 2 - tap_row + row_count, 2 - tap_col : 2 - tap_col + col_count]
        for tap_row in range(3)
        for tap_col in range(3)
    ]
    return jnp.stack(pieces, axis=2).reshape(row_count * col_count, 9, -1)


def apply_weights(patches, weight):
    return lax.dot_general(
        patches, weight, (((1,), (1,)), ((), ())), preferred_element_type=jnp.float32
    )


def weight_grad(gate_grad, patches):
    return lax.dot_general(
        gate_grad, patches, (((0,), (0,)), ((), ())), preferred_element_type=jnp.float32
    )


def spread_back(grad_taps, weight):
    taps_weight = weight.reshape(weight.shape[0], 9, -1)
    return jnp.einsum("nkg,gkc->nc", grad_taps, taps_weight, preferred_element_type=jnp.float32)


def extend_rows(field, axis):
    extent = field.shape[axis]
    last_row = lax.slice_in_dim(field, extent - 1, extent, axis=axis)
    first_row = lax.slice_in_dim(field, 0, 1, axis=axis)
    above = from_behind(last_row, "band", 1)
    below = from_behind(first_row, "band", -1)
    return jnp.concatenate([above, field, below], axis=axis)


def extend_grads(field):
    above = from_behind(field[-1:], "band", 1)
    below = from_behind(field[:1], "band", -1)
    return jnp.concatenate([above, field, below], axis=0)


def adam_update(weight, moment_one, moment_two, grad, rate):
    first_new = beta_first * moment_one + (1.0 - beta_first) * grad
    second_new = beta_second * moment_two + (1.0 - beta_second) * grad * grad
    scale_one = 1.0 - beta_first**STEP
    scale_two = 1.0 - beta_second**STEP
    direction = first_new / scale_one / (jnp.sqrt(second_new / scale_two) + adam_epsilon)
    fresh = weight - rate * (direction + weight_decay * weight)
    return (fresh, first_new, second_new, fresh.astype(jnp.bfloat16))


def by_rows(
    frames,
    grid_size,
    out_grad,
    enc_hidden,
    enc_hidden_m,
    enc_hidden_v,
    fore_hidden,
    fore_hidden_m,
    fore_hidden_v,
    enc_input,
    enc_input_m,
    enc_input_v,
    cell_vectors,
    vectors_m,
    vectors_v,
):
    device_place = lax.axis_index("band")
    row_count = frames.shape[2]
    width = HID
    gate_count = 4 * width
    col_count = out_grad.shape[3] // width
    channels = frames.shape[3] // col_count
    row_start = device_place * row_count
    cell_total = row_count * col_count
    row_ids = row_start + lax.iota(jnp.int32, row_count)
    col_ids = lax.iota(jnp.int32, col_count)
    inside = (row_ids[:, None] < grid_size[0, 0]) & (col_ids[None, :] < grid_size[0, 1])
    cell_mask = inside.astype(jnp.float32).reshape(cell_total, 1)
    frame_cells = frames[0].reshape(FRAMES_IN, row_count, col_count, channels)
    inputs_masked = jnp.where(inside[None, :, :, None], frame_cells, jnp.zeros_like(frame_cells))
    inputs_rimmed = extend_rows(inputs_masked, 1)
    copies = (
        enc_hidden.astype(jnp.bfloat16),
        fore_hidden.astype(jnp.bfloat16),
        enc_input.astype(jnp.bfloat16),
        cell_vectors.astype(jnp.bfloat16),
    )
    w_enc, w_fore, w_input, vector_all = (
        lax.all_gather(copies[0], "band", axis=0, tiled=True),
        lax.all_gather(copies[1], "band", axis=0, tiled=True),
        lax.all_gather(copies[2], "band", axis=0, tiled=True),
        lax.all_gather(copies[3], "band", axis=0, tiled=True),
    )
    vector_enc = vector_all[: 7 * width].astype(jnp.float32)
    vector_fore = vector_all[7 * width :].astype(jnp.float32)

    def enc_forward(carry, input_rim):
        hidden, state = carry
        hidden_pad = pad_columns(extend_rows(hidden, 0))
        input_pad = pad_columns(input_rim)
        conv = apply_weights(forward_taps(hidden_pad, row_count, col_count), w_enc) + apply_weights(
            forward_taps(input_pad, row_count, col_count), w_input
        )
        out_hidden, out_state = cell_math(conv, state, vector_enc, cell_mask)
        new_hidden = out_hidden.astype(jnp.bfloat16).reshape(row_count, col_count, width)
        return ((new_hidden, out_state), (hidden_pad, state))

    zero_hidden = jnp.zeros((row_count, col_count, width), jnp.bfloat16)
    zero_state = jnp.zeros((cell_total, width), jnp.float32)
    (start_hidden, start_state), (enc_pads, enc_states) = lax.scan(
        enc_forward, (zero_hidden, zero_state), inputs_rimmed
    )

    def fore_forward(carry, unused):
        hidden, state = carry
        hidden_pad = pad_columns(extend_rows(hidden, 0))
        conv = apply_weights(forward_taps(hidden_pad, row_count, col_count), w_fore)
        out_hidden, out_state = cell_math(conv, state, vector_fore, cell_mask)
        new_hidden = out_hidden.astype(jnp.bfloat16).reshape(row_count, col_count, width)
        return ((new_hidden, out_state), (hidden_pad, state, new_hidden))

    _, (fore_pads, fore_states, fore_outputs) = lax.scan(
        fore_forward, (start_hidden, start_state), None, length=FRAMES_OUT
    )
    out_cot = out_grad[0].reshape(FRAMES_OUT, cell_total, width)

    def fore_backward(carry, inputs):
        hidden_grad, state_grad, weight_sum, vector_sum = carry
        hidden_pad, state_prev, cot_step = inputs
        total_grad = hidden_grad + cot_step.astype(jnp.float32)
        patches = forward_taps(hidden_pad, row_count, col_count)
        conv = apply_weights(patches, w_fore)
        _, pull = jax.vjp(
            lambda conv_in, state_in, vector_in: cell_math(conv_in, state_in, vector_in, cell_mask),
            conv,
            state_prev,
            vector_fore,
        )
        conv_grad, prev_grad, vector_grad = pull((total_grad, state_grad))
        gate_grad = conv_grad.astype(jnp.bfloat16)
        grad_pad = pad_columns(extend_grads(gate_grad.reshape(row_count, col_count, gate_count)))
        back_hidden = spread_back(backward_taps(grad_pad, row_count, col_count), w_fore)
        step_weight = weight_grad(gate_grad, patches)
        return ((back_hidden, prev_grad, weight_sum + step_weight, vector_sum + vector_grad), None)

    fore_init = (
        jnp.zeros((cell_total, width), jnp.float32),
        jnp.zeros((cell_total, width), jnp.float32),
        jnp.zeros((gate_count, 9 * width), jnp.float32),
        jnp.zeros((7 * width,), jnp.float32),
    )
    (enc_hidden_grad, enc_state_grad, fore_weight_grad, fore_vector_grad), _ = lax.scan(
        fore_backward, fore_init, (fore_pads, fore_states, out_cot), reverse=True
    )

    def enc_backward(carry, inputs):
        hidden_grad, state_grad, weight_sum, input_sum, vector_sum = carry
        hidden_pad, input_rim, state_prev = inputs
        input_pad = pad_columns(input_rim)
        hidden_patches = forward_taps(hidden_pad, row_count, col_count)
        input_patches = forward_taps(input_pad, row_count, col_count)
        conv = apply_weights(hidden_patches, w_enc) + apply_weights(input_patches, w_input)
        _, pull = jax.vjp(
            lambda conv_in, state_in, vector_in: cell_math(conv_in, state_in, vector_in, cell_mask),
            conv,
            state_prev,
            vector_enc,
        )
        conv_grad, prev_grad, vector_grad = pull((hidden_grad, state_grad))
        gate_grad = conv_grad.astype(jnp.bfloat16)
        grad_pad = pad_columns(extend_grads(gate_grad.reshape(row_count, col_count, gate_count)))
        grad_taps = backward_taps(grad_pad, row_count, col_count)
        back_hidden = spread_back(grad_taps, w_enc)
        back_input = spread_back(grad_taps, w_input) * cell_mask
        step_weight = weight_grad(gate_grad, hidden_patches)
        step_input = weight_grad(gate_grad, input_patches)
        return (
            (
                back_hidden,
                prev_grad,
                weight_sum + step_weight,
                input_sum + step_input,
                vector_sum + vector_grad,
            ),
            back_input,
        )

    enc_init = (
        enc_hidden_grad,
        enc_state_grad,
        jnp.zeros((gate_count, 9 * width), jnp.float32),
        jnp.zeros((gate_count, 9 * channels), jnp.float32),
        jnp.zeros((7 * width,), jnp.float32),
    )
    (_, _, enc_weight_grad, input_weight_grad, enc_vector_grad), input_grads = lax.scan(
        enc_backward, enc_init, (enc_pads, inputs_rimmed, enc_states), reverse=True
    )
    hidden_block = fore_outputs.reshape(FRAMES_OUT, row_count, col_count * width)
    input_block = input_grads.reshape(FRAMES_IN, row_count, col_count * channels)
    vector_grad_all = jnp.concatenate([enc_vector_grad, fore_vector_grad])
    shares = (
        *sent_together(
            (
                enc_weight_grad.astype(jnp.bfloat16),
                fore_weight_grad.astype(jnp.bfloat16),
                input_weight_grad.astype(jnp.bfloat16),
            ),
            "band",
            0,
            1,
        ),
        summed_on_arrival(vector_grad_all.astype(jnp.bfloat16), "band", 0),
    )
    enc_share, fore_share, input_share, vector_share = (
        lax.psum(shares[0].astype(jnp.bfloat16), "grp").astype(jnp.float32),
        lax.psum(shares[1].astype(jnp.bfloat16), "grp").astype(jnp.float32),
        lax.psum(shares[2].astype(jnp.bfloat16), "grp").astype(jnp.float32),
        lax.psum(shares[3].astype(jnp.bfloat16), "grp").astype(jnp.float32),
    )
    enc_new, enc_one, enc_two, enc_copy = adam_update(
        enc_hidden, enc_hidden_m, enc_hidden_v, enc_share, matrix_rate
    )
    fore_new, fore_one, fore_two, fore_copy = adam_update(
        fore_hidden, fore_hidden_m, fore_hidden_v, fore_share, matrix_rate
    )
    input_new, input_one, input_two, input_copy = adam_update(
        enc_input, enc_input_m, enc_input_v, input_share, matrix_rate
    )
    vector_new, vector_one, vector_two, vector_copy = adam_update(
        cell_vectors, vectors_m, vectors_v, vector_share, vector_rate
    )
    return (
        hidden_block[None],
        input_block[None],
        enc_new,
        enc_one,
        enc_two,
        enc_copy,
        fore_new,
        fore_one,
        fore_two,
        fore_copy,
        input_new,
        input_one,
        input_two,
        input_copy,
        vector_new,
        vector_one,
        vector_two,
        vector_copy,
    )


f32 = jnp.float32
bf16 = jnp.bfloat16

GRID_ROWS = 16
STRIP = 16
FRAME_COLS = 80
OWN = 32
REACH = 10
REACH_MID = 5
KEPT = STRIP + 2 * REACH
ENC_REACH = 6
ENC_KEPT = STRIP + 2 * ENC_REACH
ENC_COLS = (3, 77)
PIECE_ROWS = 80
PIECE_LANES = 1408
ENC_RUNS = ((1, 28, 24), (3, 26, 23))
FORE_RUNS = ((0, 24, 22), (2, 22, 20), (5, 19, 18), (7, 17, 17), (10, 14, 22), (12, 12, 20))
LATE_RUNS = ((0, 10, 18), (2, 8, 16), (5, 5, 13), (7, 3, 11))
EARLY_RUNS = ((0, 10, 18), (2, 8, 16))
ENC_BACK_RUNS = ((0, 5, 13), (2, 3, 11))
MIB = 1024 * 1024
LARGE, LONG, MIDDLE, SMALL = 60, 56, 52, 24


def cells(first, count):
    return pl.ds(pl.multiple_of(first * GRID_ROWS, GRID_ROWS), count * GRID_ROWS)


def gate(value):
    return 0.5 * jnp.tanh(0.5 * value) + 0.5


def row_moves(value):
    total = value.shape[0]
    row = lax.broadcasted_iota(jnp.int32, value.shape, 0) & (GRID_ROWS - 1)
    above = jnp.where(row == 0, 0.0, pltpu.roll(value, 1, 0))
    below = jnp.where(row == GRID_ROWS - 1, 0.0, pltpu.roll(value, total - 1, 0))
    return above, below


def own_column():
    return STRIP * (2 * lax.axis_index("z") + lax.axis_index("core"))


def runs_of(runs, steps, step_id, run):
    for k, (first, halo, piece) in enumerate(runs):
        end = runs[k + 1][0] if k + 1 < len(runs) else steps
        pl.when((step_id >= first) & (step_id < end))(functools.partial(run, first, halo, piece))


def fill_mask(lim_ref, mask_ref, first_col):
    shape = mask_ref.shape
    place = lax.broadcasted_iota(jnp.int32, shape, 0)
    row = place & (GRID_ROWS - 1)
    col = (place >> 4) + (own_column() + first_col)
    inside = (row < lim_ref[0, 0]) & (col >= 0) & (col < lim_ref[0, 1])
    mask_ref[...] = jnp.where(inside, 1.0, 0.0)


def tile_rows(first, count):
    return slice(first * GRID_ROWS, (first + count) * GRID_ROWS)


def cuts(first, last, size, inner=()):
    edges = sorted({first, last, *[edge for edge in inner if first < edge < last]})
    pieces = []
    for lo, hi in zip(edges[:-1], edges[1:]):
        while lo < hi:
            pieces.append((lo, min(size, hi - lo)))
            lo += size
    return pieces


def cell_piece(z_ref, next_ref, c_ref, mask_ref, vec, sav_ref, lo, col, count, kept, last):
    here = tile_rows(col, count)
    z_here = tile_rows(col - lo, count)
    c_old = c_ref[here, :]
    gate_in = gate(z_ref[z_here, 0:128] + vec[0] + vec[4] * c_old)
    gate_keep = gate(z_ref[z_here, 128:256] + vec[1] + vec[5] * c_old)
    cand = jnp.tanh(z_ref[z_here, 256:384] + vec[2])
    c_new = mask_ref[here, :] * (gate_keep * c_old + gate_in * cand)
    gate_out = gate(z_ref[z_here, 384:512] + vec[3] + vec[6] * c_new)
    h_new = gate_out * jnp.tanh(c_new)
    c_ref[here, :] = c_new
    above, below = row_moves(h_new)
    next_ref[here, 0:128] = above.astype(bf16)
    next_ref[here, 128:256] = h_new.astype(bf16)
    next_ref[here, 256:384] = below.astype(bf16)
    if kept <= col < last:
        slot = tile_rows(col - kept, count)
        sav_ref[0, slot, 0:128] = gate_in
        sav_ref[0, slot, 128:256] = gate_keep
        sav_ref[0, slot, 256:384] = cand
        sav_ref[0, slot, 384:512] = gate_out
        sav_ref[0, slot, 512:640] = c_old


def forward_step(refs, lo, hi, size, kept, last, conv, aside=None):
    z_ref, h3_ref, next_ref, c_ref, mask_ref, vec_ref, sav_ref = refs
    vec = [vec_ref[k : k + 1, :] for k in range(7)]

    def cell_of(col, count):
        for piece in cuts(col, col + count, 4, (kept, last)):
            cell_piece(z_ref, next_ref, c_ref, mask_ref, vec, sav_ref, lo, *piece, kept, last)

    waiting = None
    pieces = cuts(lo, hi, size)
    for k, piece in enumerate(pieces):
        conv(*piece)
        if aside is not None:
            aside(k, len(pieces))
        if waiting is not None:
            cell_of(*waiting)
        waiting = piece
    cell_of(*waiting)
    h3_ref[tile_rows(lo, hi - lo), :] = next_ref[tile_rows(lo, hi - lo), :]


def hidden_conv(h3_ref, w_ref, z_ref, lo, extra=None, x_lo=0):
    def conv(col, count):
        taps = [h3_ref[tile_rows(col + b - 1, count), :] for b in range(3)]
        z = jnp.dot(jnp.concatenate(taps, axis=1), w_ref[...], preferred_element_type=f32)
        if extra is not None:
            x_ref, wx_ref = extra
            z = z + jnp.dot(
                x_ref[tile_rows(col - x_lo, count), :], wx_ref[...], preferred_element_type=f32
            )
        z_ref[tile_rows(col - lo, count), :] = z

    return conv


def fill_forward(w_ref, wt_ref):
    for b in range(3):
        for a in range(3):
            lanes = slice((3 * a + b) * HID, (3 * a + b + 1) * HID)
            wt_ref[(3 * b + a) * HID : (3 * b + a + 1) * HID, :] = w_ref[:, lanes].T


def frame_parts(frame):
    rest = 2048 - PIECE_LANES
    return ((0, 2 * frame, 0, PIECE_LANES), (PIECE_LANES, 10 + frame // 2 * 2, frame % 2 * rest, rest))


def pack_kernel(w_ref, wx_ref, frames_ref, vec_ref, out_ref, block_ref):
    share = w_ref.shape[0]
    out_ref[0:share, 0:1152] = w_ref[...].astype(bf16)
    out_ref[0:share, 1152:1408] = jnp.zeros((share, 256), bf16)
    out_ref[0:share, 1152:1296] = wx_ref[...].astype(bf16)
    block_ref[...] = jnp.zeros_like(block_ref)
    count = vec_ref.shape[1]
    block_ref[0:1, 768 : 768 + count] = vec_ref[...]
    near, far = block_ref[0:1, 768:896], block_ref[0:1, 896:1024]
    lane = lax.broadcasted_iota(jnp.int32, near.shape, 1)
    shift = HID - count // 2
    block_ref[14:15, 640:768] = near
    block_ref[15:16, 640:768] = jnp.where(lane < shift, pltpu.roll(near, shift, 1), pltpu.roll(far, shift, 1))
    for frame in range(FRAMES_IN):
        for lane, row, place, count in frame_parts(frame):
            block_ref[row : row + 2, place : place + count] = frames_ref[frame, :, lane : lane + count].astype(f32)
    out_ref[share : share + block_ref.shape[0], :] = block_ref[...].astype(bf16)


def copy_windows(cot_ref, frame, out_ref, place, reach):
    width = STRIP + 2 * reach
    for band in range(8):
        lo = STRIP * band - reach
        first, last = max(lo, 0), min(lo + width, 128)
        out_ref[band, place + first - lo : place + last - lo] = cot_ref[frame, first:last]
        if first > lo:
            out_ref[band, place : place + first - lo] = cot_ref[frame, 0 : first - lo]
        if last < lo + width:
            out_ref[band, place + last - lo : place + width] = cot_ref[frame, 0 : lo + width - last]


def windows_kernel(cot_ref, first_ref, second_ref):
    for k in range(2):
        copy_windows(cot_ref, 4 - k, first_ref, KEPT * k, REACH)
    for k in range(FRAMES_IN):
        copy_windows(cot_ref, 2 * FRAMES_IN + k, first_ref, KEPT * (2 + k), REACH)
        copy_windows(cot_ref, FRAMES_IN + k, first_ref, MID_COLS * (MID_PLACE + k), REACH_MID)
    for k in range(3):
        copy_windows(cot_ref, 2 - k, second_ref, KEPT * (SECOND_PLACE + k), REACH)


def fill_frames(lim_ref, mine_ref, other_ref, line_ref, vec_ref, wide_ref, pairs_ref, pair_ref):
    core_here = lax.axis_index("core")
    wide_ref[...] = jnp.zeros_like(wide_ref)
    pair_ref[...] = jnp.zeros_like(pair_ref)
    for k in range(4):
        chip = (lax.axis_index("z") - k) & 3
        for source, core in ((mine_ref, core_here), (other_ref, 1 - core_here)):
            band = 2 * chip + core
            first = k * PIECE_ROWS + HID // 2
            block = source[first : first + 16, :].astype(f32)
            for frame in range(FRAMES_IN):
                for lane, row, place, count in frame_parts(frame):
                    start = OWN * 16 + lane
                    wide_ref[band, frame, :, start : start + count] = block[row : row + 2, place : place + count]
            pairs_ref[band] = block[14:16, 640 : 640 + HID]
    for band in range(8):
        pair_ref[2 * band : 2 * band + 2, :] = pairs_ref[band]
    lanes = FRAME_COLS * 16
    row = lax.broadcasted_iota(jnp.int32, (GRID_ROWS, lanes), 0)
    col = (lax.broadcasted_iota(jnp.int32, (GRID_ROWS, lanes), 1) >> 4) + (own_column() - OWN)
    inside = (row < lim_ref[0, 0]) & (col >= 0) & (col < lim_ref[0, 1])
    start = pl.multiple_of(16 * own_column(), 256)
    for frame in range(FRAMES_IN):
        for band in range(8):
            line_ref[frame, 1, 2 * band : 2 * band + 2, :] = wide_ref[band, frame, :, pl.ds(start, lanes)]
        field = jnp.where(inside, line_ref[frame, 1], 0.0)
        above, below = row_moves(field)
        line_ref[frame, 0] = above
        line_ref[frame, 1] = field
        line_ref[frame, 2] = below
    lane = lax.broadcasted_iota(jnp.int32, (1, HID), 1)
    for k in range(14):
        at, offset = divmod(HID * k, 112)
        line = pltpu.roll(pair_ref[at : at + 1, :], (HID - offset) % HID, 1)
        filled = 112 - offset
        follow = pltpu.roll(pair_ref[at + 1 : at + 2, :], filled, 1)
        line = jnp.where(lane < filled, line, follow)
        if filled + 112 < HID:
            third = pltpu.roll(pair_ref[at + 2 : at + 3, :], (filled + 112) % HID, 1)
            line = jnp.where(lane < filled + 112, line, third)
        place = k + k // 7
        vec_ref[place : place + 1, :] = line
    vec_ref[7:8, :] = jnp.zeros((1, HID), f32)
    vec_ref[15:16, :] = jnp.zeros((1, HID), f32)


def taps_of(line_ref, frame, out_ref, first, count):
    lane = lax.broadcasted_iota(jnp.int32, (GRID_ROWS, 128), 1)
    for col in range(first, first + count):
        block, offset = divmod(16 * (col - 1), 128)
        pieces = []
        for a in range(3):
            line = line_ref[frame, a, :, 128 * block : 128 * block + 128]
            if offset + 48 > 128:
                line = jnp.where(
                    lane >= offset, line, line_ref[frame, a, :, 128 * block + 128 : 128 * block + 256]
                )
            pieces.append(pltpu.roll(line, ((64 if a == 1 else 0) - offset) % 128, 1))
        left = jnp.where(lane < 48, pieces[0], jnp.where((lane >= 64) & (lane < 112), pieces[1], 0.0))
        right = jnp.where(lane < 48, pieces[2], 0.0)
        place = tile_rows(col - ENC_COLS[0], 1)
        out_ref[place, 0:128] = left.astype(bf16)
        out_ref[place, 128:256] = right.astype(bf16)


def assemble(mine_ref, other_ref, w_ref, wx_ref=None):
    part = HID // 2
    core_here = lax.axis_index("core")
    for k in range(4):
        chip = (lax.axis_index("z") - k) & 3
        for source, core in ((mine_ref, core_here), (other_ref, 1 - core_here)):
            place = pl.ds(pl.multiple_of((2 * chip + core) * part, part), part)
            first = k * (source.shape[0] // 4)
            w_ref[place, :] = source[first : first + part, 0:1152]
            if wx_ref is not None:
                wx_ref[place, :] = source[first : first + part, 1152:1408]


def enc_kernel(
    lim_ref, mine_ref, other_ref, move_f_ref, move_b_ref,
    sav_ref, h3s_ref, own_ref, h3_ref, c_ref, w_ref, wxb_ref, vec_ref,
    wt_ref, wx_ref, wxt_ref, z_ref, next_ref, mask_ref, line_ref, taps_ref, taps_next, wide_ref, pairs_ref, pair_ref,
):
    step_id = pl.program_id(0)
    lo, hi = ENC_COLS
    kept = OWN - ENC_REACH
    last = kept + ENC_KEPT
    refs = (z_ref, h3_ref, next_ref, c_ref, mask_ref, vec_ref, sav_ref)

    @pl.when(step_id == 0)
    def _():
        h3_ref[...] = jnp.zeros_like(h3_ref)
        c_ref[...] = jnp.zeros_like(c_ref)
        fill_mask(lim_ref, mask_ref, -OWN)
        fill_frames(lim_ref, mine_ref, other_ref, line_ref, vec_ref, wide_ref, pairs_ref, pair_ref)
        assemble(mine_ref, other_ref, w_ref, wx_ref)
        fill_forward(w_ref, wt_ref)
        wx = wx_ref[...]
        wxt_ref[...] = lax.dot_general(
            move_f_ref[...], wx, (((0,), (1,)), ((), ())), preferred_element_type=f32
        ).astype(bf16)
        wxb_ref[...] = jnp.dot(wx, move_b_ref[...], preferred_element_type=f32).astype(bf16)
        taps_of(line_ref, 0, taps_ref, lo, hi - lo)

    own_ref[0] = taps_ref[tile_rows(OWN - lo, STRIP), :]

    def next_taps(k, parts):
        pieces = cuts(lo, hi, -(-(hi - lo) // parts))
        taps_of(line_ref, jnp.minimum(step_id + 1, FRAMES_IN - 1), taps_next, *pieces[k])

    @pl.when(step_id == 0)
    def _():
        def conv(col, count):
            here = tile_rows(col - lo, count)
            z_ref[here, :] = jnp.dot(taps_ref[here, :], wxt_ref[...], preferred_element_type=f32)

        forward_step(refs, lo, hi, 25, kept, last, conv, next_taps)

    @pl.when(step_id > 0)
    def _():
        h3s_ref[0] = h3_ref[pl.ds((OWN - 1) * GRID_ROWS, (STRIP + 2) * GRID_ROWS), :]

    def run(_, halo, piece):
        first, end = OWN - halo, OWN + STRIP + halo
        conv = hidden_conv(h3_ref, wt_ref, z_ref, first, (taps_ref, wxt_ref), lo)
        forward_step(refs, first, end, piece, kept, last, conv, next_taps)

    runs_of(ENC_RUNS, FRAMES_IN, step_id, run)
    taps_ref[...] = taps_next[...]


def fore_kernel(
    lim_ref, mine_ref, other_ref, vec_ref, h3_in, c_in, order_ref, out_in,
    sav_ref, mid_ref, h3s_ref, out_ref, w_ref, h3_ref, c_ref, wt_ref, z_ref, next_ref, mask_ref,
):
    step_id = pl.program_id(0)

    @pl.when(step_id == 0)
    def _():
        h3_ref[...] = h3_in[...]
        c_ref[...] = c_in[...]
        fill_mask(lim_ref, mask_ref, -OWN)
        assemble(mine_ref, other_ref, w_ref)
        fill_forward(w_ref, wt_ref)

    h3s_ref[0] = h3_ref[pl.ds((OWN - 1) * GRID_ROWS, (STRIP + 2) * GRID_ROWS), :]

    def run(first, halo, piece):
        middle = FRAMES_IN <= first < 2 * FRAMES_IN
        reach = REACH_MID if middle else REACH
        save = mid_ref if middle else sav_ref
        refs = (z_ref, h3_ref, next_ref, c_ref, mask_ref, vec_ref, save)
        lo, hi = OWN - halo, OWN + STRIP + halo
        conv = hidden_conv(h3_ref, wt_ref, z_ref, lo)
        forward_step(refs, lo, hi, piece, OWN - reach, OWN + STRIP + reach, conv)

    runs_of(FORE_RUNS, FRAMES_OUT, step_id, run)
    own = h3_ref[pl.ds(OWN * GRID_ROWS, STRIP * GRID_ROWS), 128:256]
    rows = jnp.dot(order_ref[...], own, preferred_element_type=f32).astype(bf16)
    for band in range(8):
        out_ref[band] = rows[32 * band : 32 * band + 32]


def join_kernel(got_ref, out_ref):
    for band in range(8):
        for k in range(3):
            out_ref[k, 32 * band : 32 * band + 32] = got_ref[band, 32 * k : 32 * k + 32]


def back_piece(refs, vec, col, count, own, kept):
    sav_ref, og_ref, dh_ref, dc_ref, d_ref, mask_ref, sum_ref = refs
    here = tile_rows(col, count)
    then = tile_rows(col - kept, count)
    gate_in = sav_ref[0, then, 0:128]
    gate_keep = sav_ref[0, then, 128:256]
    cand = sav_ref[0, then, 256:384]
    gate_out = sav_ref[0, then, 384:512]
    c_old = sav_ref[0, then, 512:640]
    mask = mask_ref[here, :]
    dh = dh_ref[here, :]
    if og_ref is not None:
        dh = dh + og_ref[then, :].astype(f32)
    c_new = mask * (gate_keep * c_old + gate_in * cand)
    bent = jnp.tanh(c_new)
    dz_out = dh * bent * gate_out * (1.0 - gate_out)
    dc = dc_ref[here, :] + dh * gate_out * (1.0 - bent * bent) + dz_out * vec[6]
    dc = dc * mask
    dz_in = dc * cand * gate_in * (1.0 - gate_in)
    dz_keep = dc * c_old * gate_keep * (1.0 - gate_keep)
    dz_cand = dc * gate_in * (1.0 - cand * cand)
    dc_ref[here, :] = dc * gate_keep + dz_in * vec[4] + dz_keep * vec[5]
    slot = tile_rows(col + 1, count)
    d_ref[slot, 0:128] = dz_in.astype(bf16)
    d_ref[slot, 128:256] = dz_keep.astype(bf16)
    d_ref[slot, 256:384] = dz_cand.astype(bf16)
    d_ref[slot, 384:512] = dz_out.astype(bf16)
    if own:
        terms = (dz_in, dz_keep, dz_cand, dz_out, dz_in * c_old, dz_keep * c_old, dz_out * c_new)
        for k, term in enumerate(terms):
            sum_ref[8 * k : 8 * k + 8, :] += jnp.sum(term.reshape(-1, 8, 128), axis=0)


def back_conv(d_ref, w_ref, dh_ref, col, count, wxb_ref=None, qx_ref=None):
    q = None
    for b in range(3):
        blocks = [w_ref[:, (3 * a + b) * HID : (3 * a + b + 1) * HID] for a in range(3)]
        if wxb_ref is not None:
            blocks.append(wxb_ref[:, b * HID : (b + 1) * HID])
        term = jnp.dot(
            d_ref[tile_rows(col + 2 - b, count), :],
            jnp.concatenate(blocks, axis=1),
            preferred_element_type=f32,
        )
        q = term if q is None else q + term
    down, _ = row_moves(q[:, 256:384])
    _, up = row_moves(q[:, 0:128])
    dh_ref[tile_rows(col, count), :] = up + q[:, 128:256] + down
    if wxb_ref is not None:
        qx_ref[tile_rows(col, count), :] = q[:, 384:512]


def spread(d_ref, w_ref, part_ref, col, count):
    part_ref[tile_rows(col, count), :] = jnp.dot(
        d_ref[tile_rows(col + 1, count), :], w_ref[...], preferred_element_type=f32
    )


def collect(part_ref, dh_ref, first, last, lo, hi):
    for col, count in cuts(first, last, 4, (lo + 1, hi - 1)):
        rows = []
        for a in range(3):
            total = None
            for b in range(3):
                source = col + 1 - b
                if source < lo or source + count > hi:
                    continue
                lanes = slice((3 * a + b) * HID, (3 * a + b + 1) * HID)
                term = part_ref[tile_rows(source, count), lanes]
                total = term if total is None else total + term
            rows.append(total)
        _, up = row_moves(rows[0])
        down, _ = row_moves(rows[2])
        dh_ref[tile_rows(col, count), :] = up + rows[1] + down


def spread_step(refs, vec_ref, w_ref, part_ref, lo, hi, own, size, kept=0):
    dh_ref, d_ref = refs[2], refs[4]
    vec = [vec_ref[k : k + 1, :] for k in range(7)]
    pieces = cuts(lo, hi, size)
    done = lo
    for k, (col, count) in enumerate(pieces):
        for place, width in cuts(col, col + count, 4, (own, own + STRIP)):
            back_piece(refs, vec, place, width, own <= place < own + STRIP, kept)
        if k > 0:
            collect(part_ref, dh_ref, done, col - 1, lo, hi)
            done = col - 1
        spread(d_ref, w_ref, part_ref, col, count)
    collect(part_ref, dh_ref, done, hi, lo, hi)


def backward_step(refs, vec_ref, w_ref, lo, hi, own, size, kept=0, extra=()):
    dh_ref, d_ref = refs[2], refs[4]
    vec = [vec_ref[k : k + 1, :] for k in range(7)]
    pieces = cuts(lo, hi, size)
    done = lo
    for k, (col, count) in enumerate(pieces):
        last = min(col + count + 1, hi)
        for place, width in cuts(done, last, 4, (own, own + STRIP)):
            back_piece(refs, vec, place, width, own <= place < own + STRIP, kept)
        done = last
        if k > 0:
            back_conv(d_ref, w_ref, dh_ref, *pieces[k - 1], *extra)
    back_conv(d_ref, w_ref, dh_ref, *pieces[-1], *extra)


def across(d_turned, fields):
    return jnp.dot(d_turned, fields, preferred_element_type=f32)


def turn(d_ref, first, out_ref):
    for g in range(4):
        out_ref[HID * g : HID * (g + 1), :] = d_ref[tile_rows(first, STRIP), HID * g : HID * (g + 1)].T


def side_rows(h3s_ref, frames):
    return jnp.concatenate(
        [
            jnp.concatenate([h3s_ref[k, tile_rows(b, STRIP), :] for k in frames], axis=0)
            for b in range(3)
        ],
        axis=1,
    )


def split_by_core(value, lanes, keep_ref, send_ref):
    share = value.shape[0] // 4
    core = lax.axis_index("core")
    for band in range(4):
        rows = value[band * share : (band + 1) * share]
        place = pl.ds(band // 2 * share, share)

        @pl.when(core == band % 2)
        def _(rows=rows, place=place):
            keep_ref[place, lanes] = rows

        @pl.when(core != band % 2)
        def _(rows=rows, place=place):
            send_ref[place, lanes] = rows


OWN_CELLS = pl.ds(REACH * GRID_ROWS, STRIP * GRID_ROWS)
EDGE_CELLS = REACH * GRID_ROWS


def back_late_kernel(
    lim_ref, w_ref, vec_ref, sav_ref, og_ref, mid_ref, og_mid_ref,
    d_out, sum_ref, dh_out, dc_out, left_ref, right_ref, dh_ref, dc_ref, d_ref, mask_ref, part_ref,
):
    step_id = pl.program_id(0)

    @pl.when(step_id == 0)
    def _():
        for ref in (d_ref, dh_ref, dc_ref, sum_ref):
            ref[...] = jnp.zeros_like(ref)
        fill_mask(lim_ref, mask_ref, -REACH)

    rest = (dh_ref, dc_ref, d_ref, mask_ref, sum_ref)

    def run(first, halo, piece):
        lo, hi = REACH - halo, REACH + STRIP + halo
        if first < FRAMES_IN:
            spread_step((sav_ref, og_ref, *rest), vec_ref, w_ref, part_ref, lo, hi, REACH, piece)
        else:
            kept = REACH - REACH_MID
            spread_step((mid_ref, og_mid_ref, *rest), vec_ref, w_ref, part_ref, lo, hi, REACH, piece, kept)

    runs_of(LATE_RUNS, 2 * FRAMES_IN, step_id, run)
    turn(d_ref, REACH + 1, d_out)

    @pl.when(step_id == 2 * FRAMES_IN - 1)
    def _():
        for k, (ref, out) in enumerate(((dh_ref, dh_out), (dc_ref, dc_out))):
            out[...] = ref[OWN_CELLS, :]
            left_ref[k] = ref[pl.ds(REACH * GRID_ROWS, EDGE_CELLS), :].astype(bf16)
            right_ref[k] = ref[pl.ds(STRIP * GRID_ROWS, EDGE_CELLS), :].astype(bf16)


def back_early_kernel(
    lim_ref, w_ref, vec_ref, sav_ref, og_ref, og_next, sum_in, dh_in, dc_in, left_in, right_in,
    d_out, sum_ref, dh_ref, dc_ref, d_ref, mask_ref, part_ref,
):
    step_id = pl.program_id(0)

    @pl.when(step_id == 0)
    def _():
        d_ref[...] = jnp.zeros_like(d_ref)
        for k, (ref, own) in enumerate(((dh_ref, dh_in), (dc_ref, dc_in))):
            ref[pl.ds(0, EDGE_CELLS), :] = left_in[k].astype(f32)
            ref[OWN_CELLS, :] = own[...]
            ref[pl.ds((REACH + STRIP) * GRID_ROWS, EDGE_CELLS), :] = right_in[k].astype(f32)
        sum_ref[...] = sum_in[...]
        fill_mask(lim_ref, mask_ref, -REACH)

    def run(first, halo, piece):
        og = og_ref if first < 2 else og_next
        refs = (sav_ref, og, dh_ref, dc_ref, d_ref, mask_ref, sum_ref)
        spread_step(refs, vec_ref, w_ref, part_ref, REACH - halo, REACH + STRIP + halo, REACH, piece)

    runs_of(EARLY_RUNS, FRAMES_IN, step_id, run)
    turn(d_ref, REACH + 1, d_out)


def enc_back_kernel(
    lim_ref, w_ref, wxb_ref, vec_ref, sav_ref, dh_in, dc_in,
    d_out, dx_ref, sum_ref, dh_ref, dc_ref, d_ref, mask_ref, qx_ref,
):
    step_id = pl.program_id(0)
    edge = REACH - ENC_REACH

    @pl.when(step_id == 0)
    def _():
        dh_ref[...] = dh_in[pl.ds(edge * GRID_ROWS, ENC_KEPT * GRID_ROWS), :]
        dc_ref[...] = dc_in[pl.ds(edge * GRID_ROWS, ENC_KEPT * GRID_ROWS), :]
        for ref in (d_ref, sum_ref, qx_ref):
            ref[...] = jnp.zeros_like(ref)
        fill_mask(lim_ref, mask_ref, -ENC_REACH)

    refs = (sav_ref, None, dh_ref, dc_ref, d_ref, mask_ref, sum_ref)

    def run(_, halo, piece):
        lo, hi = ENC_REACH - halo, ENC_REACH + STRIP + halo
        backward_step(refs, vec_ref, w_ref, lo, hi, ENC_REACH, piece, 0, (wxb_ref, qx_ref))

    runs_of(ENC_BACK_RUNS, FRAMES_IN, step_id, run)
    turn(d_ref, ENC_REACH + 1, d_out)
    own = tile_rows(ENC_REACH, STRIP)
    qx = qx_ref[own, :]
    down, up = row_moves(qx)
    total = up + pltpu.roll(qx, HID - 16, 1) + pltpu.roll(down, HID - 32, 1)
    total = total * mask_ref[own, :]
    lane = lax.broadcasted_iota(jnp.int32, total.shape, 1)
    total = jnp.where(lane < 16, total, 0.0)
    for group in range(2):
        line = jnp.zeros((GRID_ROWS, 128), f32)
        for k in range(8):
            place = (8 * group + k) * GRID_ROWS
            line = line + pltpu.roll(total[place : place + GRID_ROWS], 16 * k, 1)
        dx_ref[0, :, 128 * group : 128 * group + 128] = line


LATE = tuple(range(FRAMES_IN, FRAMES_OUT))
EARLY = tuple(range(FRAMES_IN))


def late_sums_kernel(dt_ref, h3s_ref, g_ref):
    g_ref[...] = across(dt_ref[...], side_rows(h3s_ref, LATE))


def put_sums(g, keep_ref, send_ref):
    for a in range(3):
        for b in range(3):
            lanes = slice((3 * a + b) * HID, (3 * a + b + 1) * HID)
            split_by_core(g[:, (3 * b + a) * HID : (3 * b + a + 1) * HID], lanes, keep_ref, send_ref)


def early_sums_kernel(dt_ref, h3s_ref, g_in, keep_ref, send_ref):
    g = g_in[...] + across(dt_ref[...], side_rows(h3s_ref, EARLY))
    put_sums(g.astype(bf16), keep_ref, send_ref)


def enc_sums_kernel(dt_ref, h3s_ref, x_ref, move_ref, sum_ref, sum_in, keep_ref, send_ref):
    g = across(dt_ref[:, 256:], side_rows(h3s_ref, EARLY[1:]))
    put_sums(g.astype(bf16), keep_ref, send_ref)

    fields = jnp.concatenate([x_ref[k] for k in EARLY], axis=0)
    gx = lax.dot_general(
        across(dt_ref[...], fields).astype(bf16),
        move_ref[...],
        (((1,), (1,)), ((), ())),
        preferred_element_type=f32,
    )
    lines = [
        jnp.sum(ref[8 * k : 8 * k + 8, :], axis=0, keepdims=True)
        for ref in (sum_ref, sum_in)
        for k in range(7)
    ] + [jnp.zeros((1, HID), f32)]
    lane = lax.broadcasted_iota(jnp.int32, (1, HID), 1)
    rows = []
    for k in range(16):
        at, offset = divmod(112 * k, HID)
        line = jnp.where(lane >= offset, lines[at], lines[at + 1])
        rows.append(jnp.where(lane >= 16, pltpu.roll(line, (16 - offset) % HID, 1), 0.0))
    rows = jnp.concatenate(rows, axis=0)
    gx = jnp.concatenate([gx[:, :128], gx[:, 128:] + jnp.concatenate([rows] * 16, axis=0)], axis=1)
    split_by_core(gx.astype(bf16), slice(1152, 1408), keep_ref, send_ref)


def whole_spec(array):
    return pl.BlockSpec(array.shape, lambda i: (0,) * len(array.shape))


def step_spec(shape, last=None):
    if last is None:
        return pl.BlockSpec((1, *shape), lambda i: (i, 0, 0))
    return pl.BlockSpec((1, *shape), lambda i: (last - i, 0, 0))


SMEM_SPEC = pl.BlockSpec(memory_space=pltpu.SMEM)


def cost(steps, columns, passes):
    return pl.CostEstimate(
        flops=2 * steps * columns * GRID_ROWS * 1152 * 512 * passes,
        bytes_accessed=steps * 2 * 1024 * 1024,
        transcendentals=steps * columns * GRID_ROWS * 128 * 5,
    )


def shaped(shape, dtype):
    return jax.ShapeDtypeStruct(shape, dtype)


FULL = FRAME_COLS * GRID_ROWS
SIDE = (STRIP + 2) * GRID_ROWS
ENC_WIDTH = (ENC_COLS[1] - ENC_COLS[0]) * GRID_ROWS
ENC_CELLS = ENC_KEPT * GRID_ROWS
CELLS = KEPT * GRID_ROWS
MID_COLS = STRIP + 2 * REACH_MID
MID_CELLS = MID_COLS * GRID_ROWS
MID_PLACE = 10
SECOND_PLACE = 7
FIRST_COLS = MID_COLS * (MID_PLACE + FRAMES_IN)
SECOND_COLS = KEPT * (SECOND_PLACE + 3)


def held(shape, dtype):
    return pltpu.HBM(shape, dtype)


def call(kernel, name, grid, ins, outs, scratch, estimate, aliases=None, memory=LARGE):
    def spec(pair):
        array, block = pair
        return whole_spec(array) if block is None else block

    return pl.pallas_call(
        kernel,
        grid=(grid,),
        in_specs=[spec(pair) for pair in ins],
        out_specs=[spec(pair) for pair in outs],
        out_shape=[pair[0] for pair in outs],
        scratch_shapes=scratch,
        compiler_params=pltpu.CompilerParams(
            dimension_semantics=("arbitrary",), vmem_limit_bytes=memory * MIB
        ),
        cost_estimate=estimate,
        input_output_aliases=aliases or {},
        name=name,
    )(*[pair[0] for pair in ins])


def moves():
    forward = np.zeros((256, 256), np.float32)
    backward = np.zeros((256, 384), np.float32)
    for a in range(3):
        for b in range(3):
            for k in range(16):
                forward[(3 * a + b) * 16 + k, 64 * a + 16 * b + k] = 1.0
                backward[(3 * a + b) * 16 + k, 128 * b + 16 * a + k] = 1.0
    return jnp.asarray(forward, bf16), jnp.asarray(backward, bf16)


ANY_SPEC = pl.BlockSpec(memory_space=pl.ANY)


def pack_parts(weight, weight_x, frames, vec):
    return call(
        pack_kernel,
        "pack_parts",
        1,
        [(weight, None), (weight_x, None), (frames, None), (vec, None)],
        [(shaped((PIECE_ROWS, 1408), bf16), None)],
        [pltpu.VMEM((16, PIECE_LANES), f32)],
        pl.CostEstimate(flops=0, bytes_accessed=0, transcendentals=0),
    )[0]


def cot_windows(cot):
    return call(
        windows_kernel,
        "cot_windows",
        1,
        [(cot, None)],
        [
            (shaped((8, FIRST_COLS, 2, HID), bf16), None),
            (shaped((8, SECOND_COLS, 2, HID), bf16), None),
        ],
        [],
        pl.CostEstimate(flops=0, bytes_accessed=0, transcendentals=0),
    )


def forward_enc(lim, mine, other):
    move_f, move_b = moves()
    wide = (OWN + 128 + FRAME_COLS - OWN) * 16
    return call(
        enc_kernel,
        "enc_forward",
        FRAMES_IN,
        [
            (lim, SMEM_SPEC),
            (mine, None),
            (other, None),
            (move_f, None),
            (move_b, None),
        ],
        [
            (held((FRAMES_IN, ENC_CELLS, 640), f32), step_spec((ENC_CELLS, 640))),
            (held((FRAMES_IN, SIDE, 384), bf16), step_spec((SIDE, 384))),
            (
                held((FRAMES_IN, STRIP * GRID_ROWS, 256), bf16),
                step_spec((STRIP * GRID_ROWS, 256)),
            ),
            (held((FULL, 384), bf16), None),
            (held((FULL, 128), f32), None),
            (held((512, 1152), bf16), None),
            (held((512, 384), bf16), None),
            (held((16, 128), f32), None),
        ],
        [
            pltpu.VMEM((1152, 512), bf16),
            pltpu.VMEM((512, 256), bf16),
            pltpu.VMEM((256, 512), bf16),
            pltpu.VMEM((ENC_WIDTH, 512), f32),
            pltpu.VMEM((FULL, 384), bf16),
            pltpu.VMEM((FULL, 128), f32),
            pltpu.VMEM((FRAMES_IN, 3, GRID_ROWS, FRAME_COLS * 16), f32),
            pltpu.VMEM((ENC_WIDTH, 256), bf16),
            pltpu.VMEM((ENC_WIDTH, 256), bf16),
            pltpu.VMEM((8, FRAMES_IN, 2, wide), f32),
            pltpu.VMEM((8, 2, HID), f32),
            pltpu.VMEM((24, HID), f32),
        ],
        cost(FRAMES_IN, 72, 1),
        memory=LONG,
    )


def row_order():
    order = np.zeros((256, 256), np.float32)
    for col in range(STRIP):
        for row in range(GRID_ROWS):
            order[row // 2 * 32 + col * 2 + row % 2, col * GRID_ROWS + row] = 1.0
    return jnp.asarray(order, bf16)


def forward_fore(lim, mine, other, vec, h3, state, second):
    second = second.reshape(8, SECOND_COLS * 2, HID)
    return call(
        fore_kernel,
        "fore_forward",
        FRAMES_OUT,
        [
            (lim, SMEM_SPEC),
            (mine, None),
            (other, None),
            (vec, None),
            (h3, None),
            (state, None),
            (row_order(), None),
            (second, ANY_SPEC),
        ],
        [
            (
                held((2 * FRAMES_IN, CELLS, 640), f32),
                pl.BlockSpec(
                    (1, CELLS, 640),
                    lambda i: (jnp.where(i < FRAMES_IN, i, jnp.maximum(i - FRAMES_IN, FRAMES_IN - 1)), 0, 0),
                ),
            ),
            (
                held((FRAMES_IN, MID_CELLS, 640), f32),
                pl.BlockSpec((1, MID_CELLS, 640), lambda i: (jnp.clip(i - FRAMES_IN, 0, FRAMES_IN - 1), 0, 0)),
            ),
            (held((FRAMES_OUT, SIDE, 384), bf16), step_spec((SIDE, 384))),
            (
                shaped(second.shape, bf16),
                pl.BlockSpec((8, 2 * STRIP, HID), lambda i: (0, i, 0)),
            ),
            (held((512, 1152), bf16), None),
        ],
        [
            pltpu.VMEM((FULL, 384), bf16),
            pltpu.VMEM((FULL, 128), f32),
            pltpu.VMEM((1152, 512), bf16),
            pltpu.VMEM((64 * GRID_ROWS, 512), f32),
            pltpu.VMEM((FULL, 384), bf16),
            pltpu.VMEM((FULL, 128), f32),
        ],
        cost(FRAMES_OUT, 56, 1),
        {7: 3},
        LONG,
    )


def join_hidden(got):
    out = call(
        join_kernel,
        "join_hidden",
        FRAMES_IN,
        [(got, pl.BlockSpec((8, 6 * STRIP, HID), lambda i: (0, i, 0)))],
        [
            (
                shaped((FRAMES_OUT, 2 * STRIP * 8, HID), bf16),
                pl.BlockSpec((3, 2 * STRIP * 8, HID), lambda i: (i, 0, 0)),
            )
        ],
        [],
        pl.CostEstimate(flops=0, bytes_accessed=1 << 21, transcendentals=0),
        memory=SMALL,
    )[0]
    out = out.reshape(FRAMES_OUT, STRIP * 8, 2, HID).transpose(0, 2, 1, 3)
    return out.reshape(1, FRAMES_OUT, 2, -1)


def tile_spec(cols, place):
    return pl.BlockSpec((cols * GRID_ROWS, HID), lambda i: (place(i), 0))


D_SHAPE = (512, STRIP * GRID_ROWS)


def turned(steps):
    return (
        pltpu.VMEM((512, steps * STRIP * GRID_ROWS), bf16),
        pl.BlockSpec(D_SHAPE, lambda i: (0, steps - 1 - i)),
    )


def backward_late(lim, weight, vec, saved, middle, og):
    own = STRIP * GRID_ROWS
    edge = held((2, EDGE_CELLS, 128), bf16)

    def first(i):
        return FRAMES_IN - 1 - jnp.minimum(i, FRAMES_IN - 1)

    def second(i):
        return jnp.minimum(2 * FRAMES_IN - 1 - i, FRAMES_IN - 1)

    return call(
        back_late_kernel,
        "fore_backward_late",
        2 * FRAMES_IN,
        [
            (lim, SMEM_SPEC),
            (weight, None),
            (vec, None),
            (saved, pl.BlockSpec((1, CELLS, 640), lambda i: (FRAMES_IN + first(i), 0, 0))),
            (og, tile_spec(KEPT, lambda i: 2 + first(i))),
            (middle, pl.BlockSpec((1, MID_CELLS, 640), lambda i: (second(i), 0, 0))),
            (og, tile_spec(MID_COLS, lambda i: MID_PLACE + second(i))),
        ],
        [
            turned(2 * FRAMES_IN),
            (held((56, 128), f32), None),
            (held((own, 128), f32), None),
            (held((own, 128), f32), None),
            (edge, None),
            (edge, None),
        ],
        [
            pltpu.VMEM((CELLS, 128), f32),
            pltpu.VMEM((CELLS, 128), f32),
            pltpu.VMEM((CELLS + 2 * GRID_ROWS, 512), bf16),
            pltpu.VMEM((CELLS, 128), f32),
            pltpu.VMEM((CELLS, 1152), f32),
        ],
        cost(2 * FRAMES_IN, 30, 1),
        memory=LONG,
    )


def backward_early(lim, weight, vec, saved, og, og_next, carried):
    return call(
        back_early_kernel,
        "fore_backward_early",
        FRAMES_IN,
        [
            (lim, SMEM_SPEC),
            (weight, None),
            (vec, None),
            (saved, step_spec((CELLS, 640), FRAMES_IN - 1)),
            (og, tile_spec(KEPT, lambda i: jnp.minimum(i, 1))),
            (og_next, tile_spec(KEPT, lambda i: jnp.maximum(i - 2, 0))),
            *[(array, None) for array in carried],
        ],
        [
            turned(FRAMES_IN),
            (held((56, 128), f32), None),
            (held((CELLS, 128), f32), None),
            (held((CELLS, 128), f32), None),
        ],
        [
            pltpu.VMEM((CELLS + 2 * GRID_ROWS, 512), bf16),
            pltpu.VMEM((CELLS, 128), f32),
            pltpu.VMEM((CELLS, 1152), f32),
        ],
        cost(FRAMES_IN, 36, 1),
        memory=MIDDLE,
    )


def backward_enc(lim, weight, weight_xb, vec, saved, dh, dc):
    last = FRAMES_IN - 1
    return call(
        enc_back_kernel,
        "enc_backward",
        FRAMES_IN,
        [
            (lim, SMEM_SPEC),
            (weight, None),
            (weight_xb, None),
            (vec, None),
            (saved, step_spec((ENC_CELLS, 640), last)),
            (dh, None),
            (dc, None),
        ],
        [
            turned(FRAMES_IN),
            (shaped((FRAMES_IN, GRID_ROWS, 256), f32), step_spec((GRID_ROWS, 256), last)),
            (shaped((56, 128), f32), None),
        ],
        [
            pltpu.VMEM((ENC_CELLS, 128), f32),
            pltpu.VMEM((ENC_CELLS, 128), f32),
            pltpu.VMEM((ENC_CELLS + 2 * GRID_ROWS, 512), bf16),
            pltpu.VMEM((ENC_CELLS, 128), f32),
            pltpu.VMEM((ENC_CELLS, 128), f32),
        ],
        cost(FRAMES_IN, 28, 1),
        memory=LONG,
    )


def sums_cost(frames):
    return pl.CostEstimate(
        flops=2 * frames * 256 * 512 * 1152, bytes_accessed=frames * 500000, transcendentals=0
    )


def gate_half(shape):
    return pl.BlockSpec((shape[0] // 2, shape[1]), lambda i: (i, 0))


def half_pair(shape, dtype):
    return (shaped(shape, dtype), gate_half(shape))


def late_sums(d_late, sides):
    return call(
        late_sums_kernel,
        "late_sums",
        2,
        [(d_late, gate_half(d_late.shape)), (sides, None)],
        [half_pair((512, 1152), f32)],
        [],
        sums_cost(2 * FRAMES_IN),
        memory=SMALL,
    )[0]


def early_sums(d_early, sides, g_late):
    return call(
        early_sums_kernel,
        "early_sums",
        2,
        [
            (d_early, gate_half(d_early.shape)),
            (sides, pl.BlockSpec((FRAMES_IN, SIDE, 384), lambda i: (0, 0, 0))),
            (g_late, gate_half(g_late.shape)),
        ],
        [half_pair((256, 1152), bf16), half_pair((256, 1152), bf16)],
        [],
        sums_cost(FRAMES_IN),
        memory=SMALL,
    )


def enc_sums(d_enc, sides, x_own, sums, fore_sums):
    move_f, _ = moves()
    return call(
        enc_sums_kernel,
        "enc_sums",
        2,
        [
            (d_enc, gate_half(d_enc.shape)),
            (sides, None),
            (x_own, None),
            (move_f, None),
            (sums, None),
            (fore_sums, None),
        ],
        [half_pair((256, 1408), bf16), half_pair((256, 1408), bf16)],
        [],
        sums_cost(FRAMES_IN),
        memory=SMALL,
    )


BAND = ("z", "core")


def column_tiles(got):
    return got.transpose(1, 0, 2, 3).reshape(-1, HID)


def passed(value, axis, steps):
    count = lax.axis_size(axis)
    return lax.ppermute(value, axis, [(k, (k + steps) % count) for k in range(count)])


def traded(blocks):
    chips = lax.axis_size("z")
    here, core = lax.axis_index("z"), lax.axis_index("core")
    pairs = blocks.reshape(chips, 2, *blocks.shape[1:])
    keep = lax.dynamic_index_in_dim(pairs, core, 1, keepdims=False)
    send = lax.dynamic_index_in_dim(pairs, 1 - core, 1, keepdims=False)
    other = passed(send, "core", 1)
    first = jnp.where(core == 0, keep, other)
    second = jnp.where(core == 0, other, keep)
    both = jnp.stack([first, second], axis=1)
    both = jnp.concatenate([both, both], axis=0)
    mine = lax.dynamic_slice_in_dim(both, here, chips)
    got = [mine[0]] + [passed(mine[s], "z", s) for s in range(1, chips)]
    order = jnp.stack(got[::-1] + got[::-1])
    ordered = lax.dynamic_slice_in_dim(order, chips - 1 - here, chips)
    return ordered.reshape(blocks.shape)


def grid_gather(share):
    count = lax.axis_size("grp")
    pieces = [share] + [passed(share, "grp", -s) for s in range(1, count)]
    place = lax.axis_index("grp")
    start = lax.rem(count - place, count) * share.shape[0]
    return lax.dynamic_slice_in_dim(jnp.concatenate(pieces + pieces), start, count * share.shape[0])


def chip_sum(keep, send):
    return (keep.astype(f32) + passed(send, "core", 1).astype(f32)).astype(bf16)


def slice_sum(total):
    chips = lax.axis_size("z") * lax.axis_size("grp")
    blocks = total.reshape(chips, -1, total.shape[1])
    got = lax.all_to_all(blocks, ("z", "grp"), 0, 0, tiled=True)
    return got


def arrived(got):
    return jnp.sum(got.astype(f32), axis=0)


def by_strips(
    frames,
    grid_size,
    out_grad,
    enc_hidden,
    enc_hidden_m,
    enc_hidden_v,
    fore_hidden,
    fore_hidden_m,
    fore_hidden_v,
    enc_input,
    enc_input_m,
    enc_input_v,
    cell_vectors,
    vectors_m,
    vectors_v,
):
    band = 2 * lax.axis_index("z") + lax.axis_index("core")
    part = cell_vectors.shape[0]
    pack = pack_parts(enc_hidden, enc_input, frames[0], cell_vectors.reshape(1, -1))
    pieces = [pack] + [passed(pack, "z", k) for k in range(1, 4)]
    cot = out_grad[0].reshape(FRAMES_OUT, 2, 8 * STRIP, HID).transpose(0, 2, 1, 3)
    first, second = cot_windows(cot)
    first, *pieces = lax.optimization_barrier((first, *pieces))
    mine = jnp.concatenate(pieces, axis=0)
    other = passed(mine, "core", 1)
    fore_part, mine = lax.optimization_barrier((fore_hidden.astype(bf16), mine))
    fore_pieces = [fore_part] + [passed(fore_part, "z", k) for k in range(1, 4)]
    enc_saved, enc_sides, x_own, h3, state, w_enc, weight_xb, vec = forward_enc(grid_size, mine, other)
    vec_enc, vec_fore = vec[:8], vec[8:]
    first, h3, *fore_pieces = lax.optimization_barrier((first, h3, *fore_pieces))
    fore_mine = jnp.concatenate(fore_pieces, axis=0)
    fore_other = passed(fore_mine, "core", 1)
    first_got = lax.all_to_all(first, BAND, 0, 0, tiled=True)
    fore_saved, fore_middle, fore_sides, second, w_fore = forward_fore(
        grid_size, fore_mine, fore_other, vec_fore, h3, state, second
    )
    second_got = lax.all_to_all(second, BAND, 0, 0, tiled=True)
    og = column_tiles(first_got)
    d_late, sums, dh, dc, left, right = backward_late(
        grid_size, w_fore, vec_fore, fore_saved, fore_middle, og
    )
    from_left = from_behind(right, BAND, 1)
    from_right = from_behind(left, BAND, -1)
    g_late = late_sums(d_late, fore_sides)
    second_got, from_right = lax.optimization_barrier((second_got, from_right))
    og_next = second_got.reshape(8, SECOND_COLS, 2, HID)[:, SECOND_PLACE * KEPT :]
    d_early, sums, dh, dc = backward_early(
        grid_size,
        w_fore,
        vec_fore,
        fore_saved,
        og,
        column_tiles(og_next),
        (sums, dh, dc, from_left, from_right),
    )
    fore_total = chip_sum(*early_sums(d_early, fore_sides, g_late))
    fore_total, dh = lax.optimization_barrier((fore_total, dh))
    fore_got = slice_sum(fore_total)
    d_enc, dx, enc_sums_of = backward_enc(grid_size, w_enc, weight_xb, vec_enc, enc_saved, dh, dc)
    keep, send = enc_sums(d_enc, enc_sides, x_own, enc_sums_of, sums)
    fore_got, keep, send, dx, second_got = lax.optimization_barrier((fore_got, keep, send, dx, second_got))
    enc_sum = chip_sum(keep, send)
    enc_sum, second_got, dx = lax.optimization_barrier((enc_sum, second_got, dx))
    enc_got = slice_sum(enc_sum)
    hidden_block, fore_got = lax.optimization_barrier((join_hidden(second_got), fore_got))
    input_got = traded(dx.reshape(FRAMES_IN, 8, 2, 256).transpose(1, 0, 2, 3))
    fore_share = grid_gather(arrived(fore_got).astype(bf16)).astype(f32)
    enc_total = arrived(enc_got)
    tail = grid_gather(enc_total.astype(bf16)).astype(f32)
    enc_share = tail[:, :1152]
    input_share = tail[:, 1152:1296]
    vector_share = lax.dynamic_slice_in_dim(enc_total[:, 1296:1408].reshape(-1), band * part, part)
    return (
        hidden_block,
        input_got.transpose(1, 2, 0, 3).reshape(1, FRAMES_IN, 2, -1),
        *adam_update(enc_hidden, enc_hidden_m, enc_hidden_v, enc_share, matrix_rate),
        *adam_update(fore_hidden, fore_hidden_m, fore_hidden_v, fore_share, matrix_rate),
        *adam_update(enc_input, enc_input_m, enc_input_v, input_share, matrix_rate),
        *adam_update(cell_vectors, vectors_m, vectors_v, vector_share, vector_rate),
    )


def solution(mesh):
    groups, bands = mesh.shape["grp"], mesh.shape["band"]

    def run(frames, grid_size, out_grad, *rest):
        strips = frames.shape[2] == GRID_ROWS and out_grad.shape[3] == STRIP * bands * HID
        strips = strips and bands == 8 and groups == 4
        if strips:
            places = Mesh(mesh.devices.reshape(groups, bands // 2, 2), ("grp", *BAND))
            body, band = by_strips, BAND
        else:
            places, body, band = mesh, by_rows, "band"
        grid = P("grp", None, band, None)
        matrix = P(band, None)
        vector = P(band)
        return jax.shard_map(
            body,
            mesh=places,
            in_specs=(grid, P("grp", None), grid, *[matrix] * 9, *[vector] * 3),
            out_specs=(grid, grid, *[matrix] * 12, *[vector] * 4),
            check_vma=False,
        )(frames, grid_size, out_grad, *rest)

    return run
```

```python
import functools

import jax
import jax.numpy as jnp
import numpy as np
from jax import lax
from jax.experimental import pallas as pl
from jax.experimental.pallas import tpu as pltpu
from jax.sharding import Mesh
from jax.sharding import PartitionSpec as P

HID = 128
FRAMES_IN = 5
FRAMES_OUT = 15
STEP = 5


beta_first = 0.5
beta_second = 0.5
adam_epsilon = 1e-08
weight_decay = 0.01
matrix_rate = 0.03
vector_rate = 0.3


def from_behind(value, axis, steps):
    count = lax.axis_size(axis)
    first, last = (max(0, -steps), min(count, count - steps))
    return lax.ppermute(value, axis, [(source, source + steps) for source in range(first, last)])


def cut_along(array, dim, peers):
    shape = array.shape
    tiles = array.reshape(*shape[:dim], peers, shape[dim] // peers, *shape[dim + 1 :])
    return jnp.moveaxis(tiles, dim, 0)


def summed_on_arrival(array, axis, dim):
    peers = lax.axis_size(axis)
    tiles = lax.all_to_all(cut_along(array, dim, peers), axis, 0, 0, tiled=True)
    return jnp.sum(tiles.astype(jnp.float32), axis=0)


def sent_together(arrays, axis, dim, along):
    widths = [a.shape[along] for a in arrays]
    both = jnp.concatenate(arrays, axis=along)
    result = summed_on_arrival(both, axis, dim)
    return tuple(jnp.split(result, [sum(widths[:k]) for k in range(1, len(widths))], axis=along))


def cell_math(conv, state_prev, vector, cell_mask):
    width = state_prev.shape[-1]
    pre_act = conv + vector[: 4 * width]
    gate_in = jax.nn.sigmoid(pre_act[..., :width] + vector[4 * width : 5 * width] * state_prev)
    gate_keep = jax.nn.sigmoid(
        pre_act[..., width : 2 * width] + vector[5 * width : 6 * width] * state_prev
    )
    candidate = jnp.tanh(pre_act[..., 2 * width : 3 * width])
    state_new = (gate_keep * state_prev + gate_in * candidate) * cell_mask
    gate_out = jax.nn.sigmoid(pre_act[..., 3 * width :] + vector[6 * width :] * state_new)
    return (gate_out * jnp.tanh(state_new), state_new)


def pad_columns(field):
    return jnp.pad(field, ((0, 0), (1, 1), (0, 0)))


def forward_taps(padded, row_count, col_count):
    pieces = [
        padded[tap_row : tap_row + row_count, tap_col : tap_col + col_count]
        for tap_row in range(3)
        for tap_col in range(3)
    ]
    return jnp.concatenate(pieces, axis=-1).reshape(row_count * col_count, -1)


def backward_taps(padded, row_count, col_count):
    pieces = [
        padded[2 - tap_row : 2 - tap_row + row_count, 2 - tap_col : 2 - tap_col + col_count]
        for tap_row in range(3)
        for tap_col in range(3)
    ]
    return jnp.stack(pieces, axis=2).reshape(row_count * col_count, 9, -1)


def apply_weights(patches, weight):
    return lax.dot_general(
        patches, weight, (((1,), (1,)), ((), ())), preferred_element_type=jnp.float32
    )


def weight_grad(gate_grad, patches):
    return lax.dot_general(
        gate_grad, patches, (((0,), (0,)), ((), ())), preferred_element_type=jnp.float32
    )


def spread_back(grad_taps, weight):
    taps_weight = weight.reshape(weight.shape[0], 9, -1)
    return jnp.einsum("nkg,gkc->nc", grad_taps, taps_weight, preferred_element_type=jnp.float32)


def extend_rows(field, axis):
    extent = field.shape[axis]
    last_row = lax.slice_in_dim(field, extent - 1, extent, axis=axis)
    first_row = lax.slice_in_dim(field, 0, 1, axis=axis)
    above = from_behind(last_row, "band", 1)
    below = from_behind(first_row, "band", -1)
    return jnp.concatenate([above, field, below], axis=axis)


def extend_grads(field):
    above = from_behind(field[-1:], "band", 1)
    below = from_behind(field[:1], "band", -1)
    return jnp.concatenate([above, field, below], axis=0)


def adam_update(weight, moment_one, moment_two, grad, rate):
    first_new = beta_first * moment_one + (1.0 - beta_first) * grad
    second_new = beta_second * moment_two + (1.0 - beta_second) * grad * grad
    scale_one = 1.0 - beta_first**STEP
    scale_two = 1.0 - beta_second**STEP
    direction = first_new / scale_one / (jnp.sqrt(second_new / scale_two) + adam_epsilon)
    fresh = weight - rate * (direction + weight_decay * weight)
    return (fresh, first_new, second_new, fresh.astype(jnp.bfloat16))


def by_rows(
    frames,
    grid_size,
    out_grad,
    enc_hidden,
    enc_hidden_m,
    enc_hidden_v,
    fore_hidden,
    fore_hidden_m,
    fore_hidden_v,
    enc_input,
    enc_input_m,
    enc_input_v,
    cell_vectors,
    vectors_m,
    vectors_v,
):
    device_place = lax.axis_index("band")
    row_count = frames.shape[2]
    width = HID
    gate_count = 4 * width
    col_count = out_grad.shape[3] // width
    channels = frames.shape[3] // col_count
    row_start = device_place * row_count
    cell_total = row_count * col_count
    row_ids = row_start + lax.iota(jnp.int32, row_count)
    col_ids = lax.iota(jnp.int32, col_count)
    inside = (row_ids[:, None] < grid_size[0, 0]) & (col_ids[None, :] < grid_size[0, 1])
    cell_mask = inside.astype(jnp.float32).reshape(cell_total, 1)
    frame_cells = frames[0].reshape(FRAMES_IN, row_count, col_count, channels)
    inputs_masked = jnp.where(inside[None, :, :, None], frame_cells, jnp.zeros_like(frame_cells))
    inputs_rimmed = extend_rows(inputs_masked, 1)
    copies = (
        enc_hidden.astype(jnp.bfloat16),
        fore_hidden.astype(jnp.bfloat16),
        enc_input.astype(jnp.bfloat16),
        cell_vectors.astype(jnp.bfloat16),
    )
    w_enc, w_fore, w_input, vector_all = (
        lax.all_gather(copies[0], "band", axis=0, tiled=True),
        lax.all_gather(copies[1], "band", axis=0, tiled=True),
        lax.all_gather(copies[2], "band", axis=0, tiled=True),
        lax.all_gather(copies[3], "band", axis=0, tiled=True),
    )
    vector_enc = vector_all[: 7 * width].astype(jnp.float32)
    vector_fore = vector_all[7 * width :].astype(jnp.float32)

    def enc_forward(carry, input_rim):
        hidden, state = carry
        hidden_pad = pad_columns(extend_rows(hidden, 0))
        input_pad = pad_columns(input_rim)
        conv = apply_weights(forward_taps(hidden_pad, row_count, col_count), w_enc) + apply_weights(
            forward_taps(input_pad, row_count, col_count), w_input
        )
        out_hidden, out_state = cell_math(conv, state, vector_enc, cell_mask)
        new_hidden = out_hidden.astype(jnp.bfloat16).reshape(row_count, col_count, width)
        return ((new_hidden, out_state), (hidden_pad, state))

    zero_hidden = jnp.zeros((row_count, col_count, width), jnp.bfloat16)
    zero_state = jnp.zeros((cell_total, width), jnp.float32)
    (start_hidden, start_state), (enc_pads, enc_states) = lax.scan(
        enc_forward, (zero_hidden, zero_state), inputs_rimmed
    )

    def fore_forward(carry, unused):
        hidden, state = carry
        hidden_pad = pad_columns(extend_rows(hidden, 0))
        conv = apply_weights(forward_taps(hidden_pad, row_count, col_count), w_fore)
        out_hidden, out_state = cell_math(conv, state, vector_fore, cell_mask)
        new_hidden = out_hidden.astype(jnp.bfloat16).reshape(row_count, col_count, width)
        return ((new_hidden, out_state), (hidden_pad, state, new_hidden))

    _, (fore_pads, fore_states, fore_outputs) = lax.scan(
        fore_forward, (start_hidden, start_state), None, length=FRAMES_OUT
    )
    out_cot = out_grad[0].reshape(FRAMES_OUT, cell_total, width)

    def fore_backward(carry, inputs):
        hidden_grad, state_grad, weight_sum, vector_sum = carry
        hidden_pad, state_prev, cot_step = inputs
        total_grad = hidden_grad + cot_step.astype(jnp.float32)
        patches = forward_taps(hidden_pad, row_count, col_count)
        conv = apply_weights(patches, w_fore)
        _, pull = jax.vjp(
            lambda conv_in, state_in, vector_in: cell_math(conv_in, state_in, vector_in, cell_mask),
            conv,
            state_prev,
            vector_fore,
        )
        conv_grad, prev_grad, vector_grad = pull((total_grad, state_grad))
        gate_grad = conv_grad.astype(jnp.bfloat16)
        grad_pad = pad_columns(extend_grads(gate_grad.reshape(row_count, col_count, gate_count)))
        back_hidden = spread_back(backward_taps(grad_pad, row_count, col_count), w_fore)
        step_weight = weight_grad(gate_grad, patches)
        return ((back_hidden, prev_grad, weight_sum + step_weight, vector_sum + vector_grad), None)

    fore_init = (
        jnp.zeros((cell_total, width), jnp.float32),
        jnp.zeros((cell_total, width), jnp.float32),
        jnp.zeros((gate_count, 9 * width), jnp.float32),
        jnp.zeros((7 * width,), jnp.float32),
    )
    (enc_hidden_grad, enc_state_grad, fore_weight_grad, fore_vector_grad), _ = lax.scan(
        fore_backward, fore_init, (fore_pads, fore_states, out_cot), reverse=True
    )

    def enc_backward(carry, inputs):
        hidden_grad, state_grad, weight_sum, input_sum, vector_sum = carry
        hidden_pad, input_rim, state_prev = inputs
        input_pad = pad_columns(input_rim)
        hidden_patches = forward_taps(hidden_pad, row_count, col_count)
        input_patches = forward_taps(input_pad, row_count, col_count)
        conv = apply_weights(hidden_patches, w_enc) + apply_weights(input_patches, w_input)
        _, pull = jax.vjp(
            lambda conv_in, state_in, vector_in: cell_math(conv_in, state_in, vector_in, cell_mask),
            conv,
            state_prev,
            vector_enc,
        )
        conv_grad, prev_grad, vector_grad = pull((hidden_grad, state_grad))
        gate_grad = conv_grad.astype(jnp.bfloat16)
        grad_pad = pad_columns(extend_grads(gate_grad.reshape(row_count, col_count, gate_count)))
        grad_taps = backward_taps(grad_pad, row_count, col_count)
        back_hidden = spread_back(grad_taps, w_enc)
        back_input = spread_back(grad_taps, w_input) * cell_mask
        step_weight = weight_grad(gate_grad, hidden_patches)
        step_input = weight_grad(gate_grad, input_patches)
        return (
            (
                back_hidden,
                prev_grad,
                weight_sum + step_weight,
                input_sum + step_input,
                vector_sum + vector_grad,
            ),
            back_input,
        )

    enc_init = (
        enc_hidden_grad,
        enc_state_grad,
        jnp.zeros((gate_count, 9 * width), jnp.float32),
        jnp.zeros((gate_count, 9 * channels), jnp.float32),
        jnp.zeros((7 * width,), jnp.float32),
    )
    (_, _, enc_weight_grad, input_weight_grad, enc_vector_grad), input_grads = lax.scan(
        enc_backward, enc_init, (enc_pads, inputs_rimmed, enc_states), reverse=True
    )
    hidden_block = fore_outputs.reshape(FRAMES_OUT, row_count, col_count * width)
    input_block = input_grads.reshape(FRAMES_IN, row_count, col_count * channels)
    vector_grad_all = jnp.concatenate([enc_vector_grad, fore_vector_grad])
    shares = (
        *sent_together(
            (
                enc_weight_grad.astype(jnp.bfloat16),
                fore_weight_grad.astype(jnp.bfloat16),
                input_weight_grad.astype(jnp.bfloat16),
            ),
            "band",
            0,
            1,
        ),
        summed_on_arrival(vector_grad_all.astype(jnp.bfloat16), "band", 0),
    )
    enc_share, fore_share, input_share, vector_share = (
        lax.psum(shares[0].astype(jnp.bfloat16), "grp").astype(jnp.float32),
        lax.psum(shares[1].astype(jnp.bfloat16), "grp").astype(jnp.float32),
        lax.psum(shares[2].astype(jnp.bfloat16), "grp").astype(jnp.float32),
        lax.psum(shares[3].astype(jnp.bfloat16), "grp").astype(jnp.float32),
    )
    enc_new, enc_one, enc_two, enc_copy = adam_update(
        enc_hidden, enc_hidden_m, enc_hidden_v, enc_share, matrix_rate
    )
    fore_new, fore_one, fore_two, fore_copy = adam_update(
        fore_hidden, fore_hidden_m, fore_hidden_v, fore_share, matrix_rate
    )
    input_new, input_one, input_two, input_copy = adam_update(
        enc_input, enc_input_m, enc_input_v, input_share, matrix_rate
    )
    vector_new, vector_one, vector_two, vector_copy = adam_update(
        cell_vectors, vectors_m, vectors_v, vector_share, vector_rate
    )
    return (
        hidden_block[None],
        input_block[None],
        enc_new,
        enc_one,
        enc_two,
        enc_copy,
        fore_new,
        fore_one,
        fore_two,
        fore_copy,
        input_new,
        input_one,
        input_two,
        input_copy,
        vector_new,
        vector_one,
        vector_two,
        vector_copy,
    )


f32 = jnp.float32
bf16 = jnp.bfloat16

GRID_ROWS = 16
STRIP = 16
FRAME_COLS = 80
OWN = 32
REACH = 10
REACH_MID = 5
KEPT = STRIP + 2 * REACH
ENC_REACH = 6
ENC_KEPT = STRIP + 2 * ENC_REACH
ENC_COLS = (3, 77)
PIECE_ROWS = 80
PIECE_LANES = 1408
ENC_RUNS = ((1, 28, 24), (3, 26, 23))
FORE_RUNS = ((0, 24, 22), (2, 22, 20), (5, 19, 18), (7, 17, 17), (10, 14, 22), (12, 12, 20))
LATE_RUNS = ((0, 10, 18), (2, 8, 16), (5, 5, 13), (7, 3, 11))
EARLY_RUNS = ((0, 10, 18), (2, 8, 16))
ENC_BACK_RUNS = ((0, 5, 13), (2, 3, 11))
MIB = 1024 * 1024
LARGE, LONG, MIDDLE, SMALL = 60, 56, 52, 24


def cells(first, count):
    return pl.ds(pl.multiple_of(first * GRID_ROWS, GRID_ROWS), count * GRID_ROWS)


def gate(value):
    return 0.5 * jnp.tanh(0.5 * value) + 0.5


def row_moves(value):
    halves = value.reshape(-1, 2, 8, HID)
    first, second = halves[:, 0], halves[:, 1]
    row = lax.broadcasted_iota(jnp.int32, first.shape, 1)
    first_down, second_down = pltpu.roll(first, 1, 1), pltpu.roll(second, 1, 1)
    first_up, second_up = pltpu.roll(first, 7, 1), pltpu.roll(second, 7, 1)
    above = [jnp.where(row == 0, 0.0, first_down), jnp.where(row == 0, first_down, second_down)]
    below = [jnp.where(row == 7, second_up, first_up), jnp.where(row == 7, 0.0, second_up)]
    return tuple(jnp.stack(pair, axis=1).reshape(value.shape) for pair in (above, below))


def own_column():
    return STRIP * (2 * lax.axis_index("z") + lax.axis_index("core"))


def runs_of(runs, steps, step_id, run):
    for k, (first, halo, piece) in enumerate(runs):
        end = runs[k + 1][0] if k + 1 < len(runs) else steps
        pl.when((step_id >= first) & (step_id < end))(functools.partial(run, first, halo, piece))


def fill_mask(lim_ref, mask_ref, first_col):
    shape = mask_ref.shape
    place = lax.broadcasted_iota(jnp.int32, shape, 0)
    row = place & (GRID_ROWS - 1)
    col = (place >> 4) + (own_column() + first_col)
    inside = (row < lim_ref[0, 0]) & (col >= 0) & (col < lim_ref[0, 1])
    mask_ref[...] = jnp.where(inside, 1.0, 0.0)


def tile_rows(first, count):
    return slice(first * GRID_ROWS, (first + count) * GRID_ROWS)


def cuts(first, last, size, inner=()):
    edges = sorted({first, last, *[edge for edge in inner if first < edge < last]})
    pieces = []
    for lo, hi in zip(edges[:-1], edges[1:]):
        while lo < hi:
            pieces.append((lo, min(size, hi - lo)))
            lo += size
    return pieces


def cell_piece(z_ref, next_ref, c_ref, mask_ref, vec, sav_ref, lo, col, count, kept, last):
    here = tile_rows(col, count)
    z_here = tile_rows(col - lo, count)
    c_old = c_ref[here, :]
    gate_in = gate(z_ref[z_here, 0:128] + vec[0] + vec[4] * c_old)
    gate_keep = gate(z_ref[z_here, 128:256] + vec[1] + vec[5] * c_old)
    cand = jnp.tanh(z_ref[z_here, 256:384] + vec[2])
    c_new = mask_ref[here, :] * (gate_keep * c_old + gate_in * cand)
    gate_out = gate(z_ref[z_here, 384:512] + vec[3] + vec[6] * c_new)
    h_new = gate_out * jnp.tanh(c_new)
    c_ref[here, :] = c_new
    above, below = row_moves(h_new)
    next_ref[here, 0:128] = above.astype(bf16)
    next_ref[here, 128:256] = h_new.astype(bf16)
    next_ref[here, 256:384] = below.astype(bf16)
    if kept <= col < last:
        slot = tile_rows(col - kept, count)
        sav_ref[0, slot, 0:128] = gate_in
        sav_ref[0, slot, 128:256] = gate_keep
        sav_ref[0, slot, 256:384] = cand
        sav_ref[0, slot, 384:512] = gate_out
        sav_ref[0, slot, 512:640] = c_old


def forward_step(refs, lo, hi, size, kept, last, conv, aside=None):
    z_ref, h3_ref, next_ref, c_ref, mask_ref, vec_ref, sav_ref = refs
    vec = [vec_ref[k : k + 1, :] for k in range(7)]

    def cell_of(col, count):
        for piece in cuts(col, col + count, 8, (kept, last)):
            cell_piece(z_ref, next_ref, c_ref, mask_ref, vec, sav_ref, lo, *piece, kept, last)

    waiting = None
    pieces = cuts(lo, hi, size)
    for k, piece in enumerate(pieces):
        conv(*piece)
        if aside is not None:
            aside(k, len(pieces))
        if waiting is not None:
            cell_of(*waiting)
        waiting = piece
    cell_of(*waiting)
    h3_ref[tile_rows(lo, hi - lo), :] = next_ref[tile_rows(lo, hi - lo), :]


def hidden_conv(h3_ref, w_ref, z_ref, lo, extra=None, x_lo=0):
    def conv(col, count):
        taps = [h3_ref[tile_rows(col + b - 1, count), :] for b in range(3)]
        z = jnp.dot(jnp.concatenate(taps, axis=1), w_ref[...], preferred_element_type=f32)
        if extra is not None:
            x_ref, wx_ref = extra
            z = z + jnp.dot(
                x_ref[tile_rows(col - x_lo, count), :], wx_ref[...], preferred_element_type=f32
            )
        z_ref[tile_rows(col - lo, count), :] = z

    return conv


def fill_forward(w_ref, wt_ref):
    for b in range(3):
        for a in range(3):
            lanes = slice((3 * a + b) * HID, (3 * a + b + 1) * HID)
            wt_ref[(3 * b + a) * HID : (3 * b + a + 1) * HID, :] = w_ref[:, lanes].T


def frame_parts(frame):
    rest = 2048 - PIECE_LANES
    return ((0, 2 * frame, 0, PIECE_LANES), (PIECE_LANES, 10 + frame // 2 * 2, frame % 2 * rest, rest))


def pack_kernel(w_ref, wx_ref, frames_ref, vec_ref, out_ref, block_ref):
    share = w_ref.shape[0]
    out_ref[0:share, 0:1152] = w_ref[...].astype(bf16)
    out_ref[0:share, 1152:1408] = jnp.zeros((share, 256), bf16)
    out_ref[0:share, 1152:1296] = wx_ref[...].astype(bf16)
    block_ref[...] = jnp.zeros_like(block_ref)
    count = vec_ref.shape[1]
    block_ref[0:1, 768 : 768 + count] = vec_ref[...]
    near, far = block_ref[0:1, 768:896], block_ref[0:1, 896:1024]
    lane = lax.broadcasted_iota(jnp.int32, near.shape, 1)
    shift = HID - count // 2
    block_ref[14:15, 640:768] = near
    block_ref[15:16, 640:768] = jnp.where(lane < shift, pltpu.roll(near, shift, 1), pltpu.roll(far, shift, 1))
    for frame in range(FRAMES_IN):
        for lane, row, place, count in frame_parts(frame):
            block_ref[row : row + 2, place : place + count] = frames_ref[frame, :, lane : lane + count].astype(f32)
    out_ref[share : share + block_ref.shape[0], :] = block_ref[...].astype(bf16)


def copy_windows(cot_ref, frame, out_ref, place, reach):
    width = STRIP + 2 * reach
    for band in range(8):
        lo = STRIP * band - reach
        first, last = max(lo, 0), min(lo + width, 128)
        out_ref[band, place + first - lo : place + last - lo] = cot_ref[frame, first:last]
        if first > lo:
            out_ref[band, place : place + first - lo] = cot_ref[frame, 0 : first - lo]
        if last < lo + width:
            out_ref[band, place + last - lo : place + width] = cot_ref[frame, 0 : lo + width - last]


def windows_kernel(cot_ref, first_ref, second_ref):
    for k in range(2):
        copy_windows(cot_ref, 4 - k, first_ref, KEPT * k, REACH)
    for k in range(FRAMES_IN):
        copy_windows(cot_ref, 2 * FRAMES_IN + k, first_ref, KEPT * (2 + k), REACH)
        copy_windows(cot_ref, FRAMES_IN + k, first_ref, MID_COLS * (MID_PLACE + k), REACH_MID)
    for k in range(3):
        copy_windows(cot_ref, 2 - k, second_ref, SECOND_PLACE + KEPT * k, REACH)


def fill_frames(lim_ref, mine_ref, other_ref, line_ref, vec_ref, wide_ref, pairs_ref, pair_ref):
    core_here = lax.axis_index("core")
    wide_ref[...] = jnp.zeros_like(wide_ref)
    pair_ref[...] = jnp.zeros_like(pair_ref)
    for k in range(4):
        chip = (lax.axis_index("z") - k) & 3
        for source, core in ((mine_ref, core_here), (other_ref, 1 - core_here)):
            band = 2 * chip + core
            first = k * PIECE_ROWS + HID // 2
            block = source[first : first + 16, :].astype(f32)
            for frame in range(FRAMES_IN):
                for lane, row, place, count in frame_parts(frame):
                    start = OWN * 16 + lane
                    wide_ref[band, frame, :, start : start + count] = block[row : row + 2, place : place + count]
            pairs_ref[band] = block[14:16, 640 : 640 + HID]
    for band in range(8):
        pair_ref[2 * band : 2 * band + 2, :] = pairs_ref[band]
    lanes = FRAME_COLS * 16
    row = lax.broadcasted_iota(jnp.int32, (GRID_ROWS, lanes), 0)
    col = (lax.broadcasted_iota(jnp.int32, (GRID_ROWS, lanes), 1) >> 4) + (own_column() - OWN)
    inside = (row < lim_ref[0, 0]) & (col >= 0) & (col < lim_ref[0, 1])
    start = pl.multiple_of(16 * own_column(), 256)
    for frame in range(FRAMES_IN):
        for band in range(8):
            line_ref[frame, 1, 2 * band : 2 * band + 2, :] = wide_ref[band, frame, :, pl.ds(start, lanes)]
        field = jnp.where(inside, line_ref[frame, 1], 0.0)
        line_ref[frame, 1] = field
        for block in range(FRAME_COLS // 8):
            part = slice(HID * block, HID * (block + 1))
            above, below = row_moves(line_ref[frame, 1, :, part])
            line_ref[frame, 0, :, part] = above
            line_ref[frame, 2, :, part] = below
    lane = lax.broadcasted_iota(jnp.int32, (1, HID), 1)
    for k in range(14):
        at, offset = divmod(HID * k, 112)
        line = pltpu.roll(pair_ref[at : at + 1, :], (HID - offset) % HID, 1)
        filled = 112 - offset
        follow = pltpu.roll(pair_ref[at + 1 : at + 2, :], filled, 1)
        line = jnp.where(lane < filled, line, follow)
        if filled + 112 < HID:
            third = pltpu.roll(pair_ref[at + 2 : at + 3, :], (filled + 112) % HID, 1)
            line = jnp.where(lane < filled + 112, line, third)
        place = k + k // 7
        vec_ref[place : place + 1, :] = line
    vec_ref[7:8, :] = jnp.zeros((1, HID), f32)
    vec_ref[15:16, :] = jnp.zeros((1, HID), f32)


def taps_of(line_ref, frame, out_ref, first, count):
    lane = lax.broadcasted_iota(jnp.int32, (GRID_ROWS, 128), 1)
    for col in range(first, first + count):
        block, offset = divmod(16 * (col - 1), 128)
        pieces = []
        for a in range(3):
            line = line_ref[frame, a, :, 128 * block : 128 * block + 128]
            if offset + 48 > 128:
                line = jnp.where(
                    lane >= offset, line, line_ref[frame, a, :, 128 * block + 128 : 128 * block + 256]
                )
            pieces.append(pltpu.roll(line, ((64 if a == 1 else 0) - offset) % 128, 1))
        left = jnp.where(lane < 48, pieces[0], jnp.where((lane >= 64) & (lane < 112), pieces[1], 0.0))
        right = jnp.where(lane < 48, pieces[2], 0.0)
        place = tile_rows(col - ENC_COLS[0], 1)
        out_ref[place, 0:128] = left.astype(bf16)
        out_ref[place, 128:256] = right.astype(bf16)


def assemble(mine_ref, other_ref, w_ref, wx_ref=None):
    part = HID // 2
    core_here = lax.axis_index("core")
    for k in range(4):
        chip = (lax.axis_index("z") - k) & 3
        for source, core in ((mine_ref, core_here), (other_ref, 1 - core_here)):
            place = pl.ds(pl.multiple_of((2 * chip + core) * part, part), part)
            first = k * (source.shape[0] // 4)
            w_ref[place, :] = source[first : first + part, 0:1152]
            if wx_ref is not None:
                wx_ref[place, :] = source[first : first + part, 1152:1408]


def enc_kernel(
    lim_ref, mine_ref, other_ref, move_f_ref, move_b_ref,
    sav_ref, h3s_ref, own_ref, h3_ref, c_ref, w_ref, wxb_ref, vec_ref,
    wt_ref, wx_ref, wxt_ref, z_ref, next_ref, mask_ref, line_ref, taps_ref, taps_next, wide_ref, pairs_ref, pair_ref,
):
    step_id = pl.program_id(0)
    lo, hi = ENC_COLS
    kept = OWN - ENC_REACH
    last = kept + ENC_KEPT
    refs = (z_ref, h3_ref, next_ref, c_ref, mask_ref, vec_ref, sav_ref)

    @pl.when(step_id == 0)
    def _():
        h3_ref[...] = jnp.zeros_like(h3_ref)
        c_ref[...] = jnp.zeros_like(c_ref)
        fill_mask(lim_ref, mask_ref, -OWN)
        fill_frames(lim_ref, mine_ref, other_ref, line_ref, vec_ref, wide_ref, pairs_ref, pair_ref)
        assemble(mine_ref, other_ref, w_ref, wx_ref)
        fill_forward(w_ref, wt_ref)
        wx = wx_ref[...]
        wxt_ref[...] = lax.dot_general(
            move_f_ref[...], wx, (((0,), (1,)), ((), ())), preferred_element_type=f32
        ).astype(bf16)
        wxb_ref[...] = jnp.dot(wx, move_b_ref[...], preferred_element_type=f32).astype(bf16)
        taps_of(line_ref, 0, taps_ref, lo, hi - lo)

    own_ref[0] = taps_ref[tile_rows(OWN - lo, STRIP), :]

    def next_taps(k, parts):
        pieces = cuts(lo, hi, -(-(hi - lo) // parts))
        taps_of(line_ref, jnp.minimum(step_id + 1, FRAMES_IN - 1), taps_next, *pieces[k])

    @pl.when(step_id == 0)
    def _():
        def conv(col, count):
            here = tile_rows(col - lo, count)
            z_ref[here, :] = jnp.dot(taps_ref[here, :], wxt_ref[...], preferred_element_type=f32)

        forward_step(refs, lo, hi, 25, kept, last, conv, next_taps)

    @pl.when(step_id > 0)
    def _():
        h3s_ref[0] = h3_ref[pl.ds((OWN - 1) * GRID_ROWS, (STRIP + 2) * GRID_ROWS), :]

    def run(_, halo, piece):
        first, end = OWN - halo, OWN + STRIP + halo
        conv = hidden_conv(h3_ref, wt_ref, z_ref, first, (taps_ref, wxt_ref), lo)
        forward_step(refs, first, end, piece, kept, last, conv, next_taps)

    runs_of(ENC_RUNS, FRAMES_IN, step_id, run)
    taps_ref[...] = taps_next[...]


def fore_kernel(
    lim_ref, mine_ref, other_ref, vec_ref, h3_in, c_in, order_ref, out_in,
    sav_ref, mid_ref, h3s_ref, out_ref, w_ref, h3_ref, c_ref, wt_ref, z_ref, next_ref, mask_ref,
):
    step_id = pl.program_id(0)

    @pl.when(step_id == 0)
    def _():
        h3_ref[...] = h3_in[...]
        c_ref[...] = c_in[...]
        fill_mask(lim_ref, mask_ref, -OWN)
        assemble(mine_ref, other_ref, w_ref)
        fill_forward(w_ref, wt_ref)

    h3s_ref[0] = h3_ref[pl.ds((OWN - 1) * GRID_ROWS, (STRIP + 2) * GRID_ROWS), :]

    def run(first, halo, piece):
        middle = FRAMES_IN <= first < 2 * FRAMES_IN
        reach = REACH_MID if middle else REACH
        save = mid_ref if middle else sav_ref
        refs = (z_ref, h3_ref, next_ref, c_ref, mask_ref, vec_ref, save)
        lo, hi = OWN - halo, OWN + STRIP + halo
        conv = hidden_conv(h3_ref, wt_ref, z_ref, lo)
        forward_step(refs, lo, hi, piece, OWN - reach, OWN + STRIP + reach, conv)

    runs_of(FORE_RUNS, FRAMES_OUT, step_id, run)
    own = h3_ref[pl.ds(OWN * GRID_ROWS, STRIP * GRID_ROWS), 128:256]
    rows = jnp.dot(order_ref[...], own, preferred_element_type=f32).astype(bf16)
    for band in range(8):
        out_ref[band] = rows[32 * band : 32 * band + 32]


def join_kernel(got_ref, out_ref):
    for band in range(8):
        for k in range(3):
            out_ref[k, 32 * band : 32 * band + 32] = got_ref[band, 32 * k : 32 * k + 32]


def back_piece(refs, vec, col, count, own, kept):
    sav_ref, og_ref, dh_ref, dc_ref, d_ref, mask_ref, sum_ref = refs
    here = tile_rows(col, count)
    then = tile_rows(col - kept, count)
    gate_in = sav_ref[0, then, 0:128]
    gate_keep = sav_ref[0, then, 128:256]
    cand = sav_ref[0, then, 256:384]
    gate_out = sav_ref[0, then, 384:512]
    c_old = sav_ref[0, then, 512:640]
    mask = mask_ref[here, :]
    dh = dh_ref[here, :]
    if og_ref is not None:
        dh = dh + og_ref[then, :].astype(f32)
    c_new = mask * (gate_keep * c_old + gate_in * cand)
    bent = jnp.tanh(c_new)
    dz_out = dh * bent * gate_out * (1.0 - gate_out)
    dc = dc_ref[here, :] + dh * gate_out * (1.0 - bent * bent) + dz_out * vec[6]
    dc = dc * mask
    dz_in = dc * cand * gate_in * (1.0 - gate_in)
    dz_keep = dc * c_old * gate_keep * (1.0 - gate_keep)
    dz_cand = dc * gate_in * (1.0 - cand * cand)
    dc_ref[here, :] = dc * gate_keep + dz_in * vec[4] + dz_keep * vec[5]
    slot = tile_rows(col + 1, count)
    d_ref[slot, 0:128] = dz_in.astype(bf16)
    d_ref[slot, 128:256] = dz_keep.astype(bf16)
    d_ref[slot, 256:384] = dz_cand.astype(bf16)
    d_ref[slot, 384:512] = dz_out.astype(bf16)
    if own:
        terms = (dz_in, dz_keep, dz_cand, dz_out, dz_in * c_old, dz_keep * c_old, dz_out * c_new)
        for k, term in enumerate(terms):
            sum_ref[8 * k : 8 * k + 8, :] += jnp.sum(term.reshape(-1, 8, 128), axis=0)


def back_conv(d_ref, w_ref, dh_ref, col, count, wxb_ref=None, qx_ref=None):
    q = None
    for b in range(3):
        blocks = [w_ref[:, (3 * a + b) * HID : (3 * a + b + 1) * HID] for a in range(3)]
        if wxb_ref is not None:
            blocks.append(wxb_ref[:, b * HID : (b + 1) * HID])
        term = jnp.dot(
            d_ref[tile_rows(col + 2 - b, count), :],
            jnp.concatenate(blocks, axis=1),
            preferred_element_type=f32,
        )
        q = term if q is None else q + term
    down, _ = row_moves(q[:, 256:384])
    _, up = row_moves(q[:, 0:128])
    dh_ref[tile_rows(col, count), :] = up + q[:, 128:256] + down
    if wxb_ref is not None:
        qx_ref[tile_rows(col, count), :] = q[:, 384:512]


def spread(d_ref, w_ref, part_ref, col, count):
    part_ref[tile_rows(col, count), :] = jnp.dot(
        d_ref[tile_rows(col + 1, count), :], w_ref[...], preferred_element_type=f32
    )


def collect(part_ref, dh_ref, first, last, lo, hi):
    for col, count in cuts(first, last, 4, (lo + 1, hi - 1)):
        rows = []
        for a in range(3):
            total = None
            for b in range(3):
                source = col + 1 - b
                if source < lo or source + count > hi:
                    continue
                lanes = slice((3 * a + b) * HID, (3 * a + b + 1) * HID)
                term = part_ref[tile_rows(source, count), lanes]
                total = term if total is None else total + term
            rows.append(total)
        _, up = row_moves(rows[0])
        down, _ = row_moves(rows[2])
        dh_ref[tile_rows(col, count), :] = up + rows[1] + down


def spread_step(refs, vec_ref, w_ref, part_ref, lo, hi, own, size, kept=0):
    dh_ref, d_ref = refs[2], refs[4]
    vec = [vec_ref[k : k + 1, :] for k in range(7)]
    pieces = cuts(lo, hi, size)
    done = lo
    for k, (col, count) in enumerate(pieces):
        for place, width in cuts(col, col + count, 4, (own, own + STRIP)):
            back_piece(refs, vec, place, width, own <= place < own + STRIP, kept)
        if k > 0:
            collect(part_ref, dh_ref, done, col - 1, lo, hi)
            done = col - 1
        spread(d_ref, w_ref, part_ref, col, count)
    collect(part_ref, dh_ref, done, hi, lo, hi)


def backward_step(refs, vec_ref, w_ref, lo, hi, own, size, kept=0, extra=()):
    dh_ref, d_ref = refs[2], refs[4]
    vec = [vec_ref[k : k + 1, :] for k in range(7)]
    pieces = cuts(lo, hi, size)
    done = lo
    for k, (col, count) in enumerate(pieces):
        last = min(col + count + 1, hi)
        for place, width in cuts(done, last, 8, (own, own + STRIP)):
            back_piece(refs, vec, place, width, own <= place < own + STRIP, kept)
        done = last
        if k > 0:
            back_conv(d_ref, w_ref, dh_ref, *pieces[k - 1], *extra)
    back_conv(d_ref, w_ref, dh_ref, *pieces[-1], *extra)


def across(d_turned, fields):
    return jnp.dot(d_turned, fields, preferred_element_type=f32)


def turn(d_ref, first, out_ref):
    for g in range(4):
        out_ref[HID * g : HID * (g + 1), :] = d_ref[tile_rows(first, STRIP), HID * g : HID * (g + 1)].T


def side_rows(h3s_ref, frames):
    return jnp.concatenate(
        [
            jnp.concatenate([h3s_ref[k, tile_rows(b, STRIP), :] for k in frames], axis=0)
            for b in range(3)
        ],
        axis=1,
    )


def split_by_core(value, lanes, keep_ref, send_ref):
    share = value.shape[0] // 4
    core = lax.axis_index("core")
    for band in range(4):
        rows = value[band * share : (band + 1) * share]
        place = pl.ds(band // 2 * share, share)

        @pl.when(core == band % 2)
        def _(rows=rows, place=place):
            keep_ref[place, lanes] = rows

        @pl.when(core != band % 2)
        def _(rows=rows, place=place):
            send_ref[place, lanes] = rows


OWN_CELLS = pl.ds(REACH * GRID_ROWS, STRIP * GRID_ROWS)
EDGE_CELLS = REACH * GRID_ROWS


def back_late_kernel(
    lim_ref, w_ref, vec_ref, sav_ref, og_ref, mid_ref, og_mid_ref,
    d_out, sum_ref, dh_out, dc_out, left_ref, right_ref, dh_ref, dc_ref, d_ref, mask_ref, part_ref,
):
    step_id = pl.program_id(0)

    @pl.when(step_id == 0)
    def _():
        for ref in (d_ref, dh_ref, dc_ref, sum_ref):
            ref[...] = jnp.zeros_like(ref)
        fill_mask(lim_ref, mask_ref, -REACH)

    rest = (dh_ref, dc_ref, d_ref, mask_ref, sum_ref)

    def run(first, halo, piece):
        lo, hi = REACH - halo, REACH + STRIP + halo
        if first < FRAMES_IN:
            spread_step((sav_ref, og_ref, *rest), vec_ref, w_ref, part_ref, lo, hi, REACH, piece)
        else:
            kept = REACH - REACH_MID
            spread_step((mid_ref, og_mid_ref, *rest), vec_ref, w_ref, part_ref, lo, hi, REACH, piece, kept)

    runs_of(LATE_RUNS, 2 * FRAMES_IN, step_id, run)
    turn(d_ref, REACH + 1, d_out)

    @pl.when(step_id == 2 * FRAMES_IN - 1)
    def _():
        for k, (ref, out) in enumerate(((dh_ref, dh_out), (dc_ref, dc_out))):
            out[...] = ref[OWN_CELLS, :]
            left_ref[k] = ref[pl.ds(REACH * GRID_ROWS, EDGE_CELLS), :].astype(bf16)
            right_ref[k] = ref[pl.ds(STRIP * GRID_ROWS, EDGE_CELLS), :].astype(bf16)


def back_early_kernel(
    lim_ref, w_ref, vec_ref, sav_ref, og_ref, og_next, sum_in, dh_in, dc_in, left_in, right_in,
    d_out, sum_ref, dh_ref, dc_ref, d_ref, mask_ref, part_ref,
):
    step_id = pl.program_id(0)

    @pl.when(step_id == 0)
    def _():
        d_ref[...] = jnp.zeros_like(d_ref)
        for k, (ref, own) in enumerate(((dh_ref, dh_in), (dc_ref, dc_in))):
            ref[pl.ds(0, EDGE_CELLS), :] = left_in[k].astype(f32)
            ref[OWN_CELLS, :] = own[...]
            ref[pl.ds((REACH + STRIP) * GRID_ROWS, EDGE_CELLS), :] = right_in[k].astype(f32)
        sum_ref[...] = sum_in[...]
        fill_mask(lim_ref, mask_ref, -REACH)

    def run(first, halo, piece):
        og = og_ref if first < 2 else og_next
        refs = (sav_ref, og, dh_ref, dc_ref, d_ref, mask_ref, sum_ref)
        spread_step(refs, vec_ref, w_ref, part_ref, REACH - halo, REACH + STRIP + halo, REACH, piece)

    runs_of(EARLY_RUNS, FRAMES_IN, step_id, run)
    turn(d_ref, REACH + 1, d_out)


def enc_back_kernel(
    lim_ref, w_ref, wxb_ref, vec_ref, sav_ref, dh_in, dc_in,
    d_out, dx_ref, sum_ref, dh_ref, dc_ref, d_ref, mask_ref, qx_ref,
):
    step_id = pl.program_id(0)
    edge = REACH - ENC_REACH

    @pl.when(step_id == 0)
    def _():
        dh_ref[...] = dh_in[pl.ds(edge * GRID_ROWS, ENC_KEPT * GRID_ROWS), :]
        dc_ref[...] = dc_in[pl.ds(edge * GRID_ROWS, ENC_KEPT * GRID_ROWS), :]
        for ref in (d_ref, sum_ref, qx_ref):
            ref[...] = jnp.zeros_like(ref)
        fill_mask(lim_ref, mask_ref, -ENC_REACH)

    refs = (sav_ref, None, dh_ref, dc_ref, d_ref, mask_ref, sum_ref)

    def run(_, halo, piece):
        lo, hi = ENC_REACH - halo, ENC_REACH + STRIP + halo
        backward_step(refs, vec_ref, w_ref, lo, hi, ENC_REACH, piece, 0, (wxb_ref, qx_ref))

    runs_of(ENC_BACK_RUNS, FRAMES_IN, step_id, run)
    turn(d_ref, ENC_REACH + 1, d_out)
    own = tile_rows(ENC_REACH, STRIP)
    qx = qx_ref[own, :]
    down, up = row_moves(qx)
    total = up + pltpu.roll(qx, HID - 16, 1) + pltpu.roll(down, HID - 32, 1)
    total = total * mask_ref[own, :]
    lane = lax.broadcasted_iota(jnp.int32, total.shape, 1)
    total = jnp.where(lane < 16, total, 0.0)
    for group in range(2):
        line = jnp.zeros((GRID_ROWS, 128), f32)
        for k in range(8):
            place = (8 * group + k) * GRID_ROWS
            line = line + pltpu.roll(total[place : place + GRID_ROWS], 16 * k, 1)
        dx_ref[0, :, 128 * group : 128 * group + 128] = line


LATE = tuple(range(FRAMES_IN, FRAMES_OUT))
EARLY = tuple(range(FRAMES_IN))


def late_sums_kernel(dt_ref, h3s_ref, g_ref):
    g_ref[...] = across(dt_ref[...], side_rows(h3s_ref, LATE))


def put_sums(g, keep_ref, send_ref):
    for a in range(3):
        for b in range(3):
            lanes = slice((3 * a + b) * HID, (3 * a + b + 1) * HID)
            split_by_core(g[:, (3 * b + a) * HID : (3 * b + a + 1) * HID], lanes, keep_ref, send_ref)


def early_sums_kernel(dt_ref, h3s_ref, g_in, keep_ref, send_ref):
    g = g_in[...] + across(dt_ref[...], side_rows(h3s_ref, EARLY))
    put_sums(g.astype(bf16), keep_ref, send_ref)


def enc_sums_kernel(dt_ref, h3s_ref, x_ref, move_ref, sum_ref, sum_in, keep_ref, send_ref):
    g = across(dt_ref[:, 256:], side_rows(h3s_ref, EARLY[1:]))
    put_sums(g.astype(bf16), keep_ref, send_ref)

    fields = jnp.concatenate([x_ref[k] for k in EARLY], axis=0)
    gx = lax.dot_general(
        across(dt_ref[...], fields).astype(bf16),
        move_ref[...],
        (((1,), (1,)), ((), ())),
        preferred_element_type=f32,
    )
    lines = [
        jnp.sum(ref[8 * k : 8 * k + 8, :], axis=0, keepdims=True)
        for ref in (sum_ref, sum_in)
        for k in range(7)
    ] + [jnp.zeros((1, HID), f32)]
    lane = lax.broadcasted_iota(jnp.int32, (1, HID), 1)
    rows = []
    for k in range(16):
        at, offset = divmod(112 * k, HID)
        line = jnp.where(lane >= offset, lines[at], lines[at + 1])
        rows.append(jnp.where(lane >= 16, pltpu.roll(line, (16 - offset) % HID, 1), 0.0))
    rows = jnp.concatenate(rows, axis=0)
    gx = jnp.concatenate([gx[:, :128], gx[:, 128:] + jnp.concatenate([rows] * 16, axis=0)], axis=1)
    split_by_core(gx.astype(bf16), slice(1152, 1408), keep_ref, send_ref)


def whole_spec(array):
    return pl.BlockSpec(array.shape, lambda i: (0,) * len(array.shape))


def step_spec(shape, last=None):
    if last is None:
        return pl.BlockSpec((1, *shape), lambda i: (i, 0, 0))
    return pl.BlockSpec((1, *shape), lambda i: (last - i, 0, 0))


SMEM_SPEC = pl.BlockSpec(memory_space=pltpu.SMEM)


def cost(steps, columns, passes):
    return pl.CostEstimate(
        flops=2 * steps * columns * GRID_ROWS * 1152 * 512 * passes,
        bytes_accessed=steps * 2 * 1024 * 1024,
        transcendentals=steps * columns * GRID_ROWS * 128 * 5,
    )


def shaped(shape, dtype):
    return jax.ShapeDtypeStruct(shape, dtype)


FULL = FRAME_COLS * GRID_ROWS
SIDE = (STRIP + 2) * GRID_ROWS
ENC_WIDTH = (ENC_COLS[1] - ENC_COLS[0]) * GRID_ROWS
ENC_CELLS = ENC_KEPT * GRID_ROWS
CELLS = KEPT * GRID_ROWS
MID_COLS = STRIP + 2 * REACH_MID
MID_CELLS = MID_COLS * GRID_ROWS
MID_PLACE = 10
SECOND_PLACE = FRAMES_OUT * STRIP
FIRST_COLS = MID_COLS * (MID_PLACE + FRAMES_IN)
SECOND_COLS = SECOND_PLACE + 3 * KEPT


def held(shape, dtype):
    return pltpu.HBM(shape, dtype)


def call(kernel, name, grid, ins, outs, scratch, estimate, aliases=None, memory=LARGE):
    def spec(pair):
        array, block = pair
        return whole_spec(array) if block is None else block

    return pl.pallas_call(
        kernel,
        grid=(grid,),
        in_specs=[spec(pair) for pair in ins],
        out_specs=[spec(pair) for pair in outs],
        out_shape=[pair[0] for pair in outs],
        scratch_shapes=scratch,
        compiler_params=pltpu.CompilerParams(
            dimension_semantics=("arbitrary",), vmem_limit_bytes=memory * MIB
        ),
        cost_estimate=estimate,
        input_output_aliases=aliases or {},
        name=name,
    )(*[pair[0] for pair in ins])


def moves():
    forward = np.zeros((256, 256), np.float32)
    backward = np.zeros((256, 384), np.float32)
    for a in range(3):
        for b in range(3):
            for k in range(16):
                forward[(3 * a + b) * 16 + k, 64 * a + 16 * b + k] = 1.0
                backward[(3 * a + b) * 16 + k, 128 * b + 16 * a + k] = 1.0
    return jnp.asarray(forward, bf16), jnp.asarray(backward, bf16)


ANY_SPEC = pl.BlockSpec(memory_space=pl.ANY)


def pack_parts(weight, weight_x, frames, vec):
    return call(
        pack_kernel,
        "pack_parts",
        1,
        [(weight, None), (weight_x, None), (frames, None), (vec, None)],
        [(shaped((PIECE_ROWS, 1408), bf16), None)],
        [pltpu.VMEM((16, PIECE_LANES), f32)],
        pl.CostEstimate(flops=0, bytes_accessed=0, transcendentals=0),
    )[0]


def cot_windows(cot):
    return call(
        windows_kernel,
        "cot_windows",
        1,
        [(cot, None)],
        [
            (shaped((8, FIRST_COLS, 2, HID), bf16), None),
            (shaped((8, SECOND_COLS, 2, HID), bf16), None),
        ],
        [],
        pl.CostEstimate(flops=0, bytes_accessed=0, transcendentals=0),
    )


def forward_enc(lim, mine, other):
    move_f, move_b = moves()
    wide = (OWN + 128 + FRAME_COLS - OWN) * 16
    return call(
        enc_kernel,
        "enc_forward",
        FRAMES_IN,
        [
            (lim, SMEM_SPEC),
            (mine, None),
            (other, None),
            (move_f, None),
            (move_b, None),
        ],
        [
            (held((FRAMES_IN, ENC_CELLS, 640), f32), step_spec((ENC_CELLS, 640))),
            (held((FRAMES_IN, SIDE, 384), bf16), step_spec((SIDE, 384))),
            (
                held((FRAMES_IN, STRIP * GRID_ROWS, 256), bf16),
                step_spec((STRIP * GRID_ROWS, 256)),
            ),
            (held((FULL, 384), bf16), None),
            (held((FULL, 128), f32), None),
            (held((512, 1152), bf16), None),
            (held((512, 384), bf16), None),
            (held((16, 128), f32), None),
        ],
        [
            pltpu.VMEM((1152, 512), bf16),
            pltpu.VMEM((512, 256), bf16),
            pltpu.VMEM((256, 512), bf16),
            pltpu.VMEM((ENC_WIDTH, 512), f32),
            pltpu.VMEM((FULL, 384), bf16),
            pltpu.VMEM((FULL, 128), f32),
            pltpu.VMEM((FRAMES_IN, 3, GRID_ROWS, FRAME_COLS * 16), f32),
            pltpu.VMEM((ENC_WIDTH, 256), bf16),
            pltpu.VMEM((ENC_WIDTH, 256), bf16),
            pltpu.VMEM((8, FRAMES_IN, 2, wide), f32),
            pltpu.VMEM((8, 2, HID), f32),
            pltpu.VMEM((24, HID), f32),
        ],
        cost(FRAMES_IN, 72, 1),
        memory=LONG,
    )


def row_order():
    order = np.zeros((256, 256), np.float32)
    for col in range(STRIP):
        for row in range(GRID_ROWS):
            order[row // 2 * 32 + col * 2 + row % 2, col * GRID_ROWS + row] = 1.0
    return jnp.asarray(order, bf16)


def forward_fore(lim, mine, other, vec, h3, state, second):
    second = second.reshape(8, SECOND_COLS * 2, HID)
    return call(
        fore_kernel,
        "fore_forward",
        FRAMES_OUT,
        [
            (lim, SMEM_SPEC),
            (mine, None),
            (other, None),
            (vec, None),
            (h3, None),
            (state, None),
            (row_order(), None),
            (second, ANY_SPEC),
        ],
        [
            (
                held((2 * FRAMES_IN, CELLS, 640), f32),
                pl.BlockSpec(
                    (1, CELLS, 640),
                    lambda i: (jnp.where(i < FRAMES_IN, i, jnp.maximum(i - FRAMES_IN, FRAMES_IN - 1)), 0, 0),
                ),
            ),
            (
                held((FRAMES_IN, MID_CELLS, 640), f32),
                pl.BlockSpec((1, MID_CELLS, 640), lambda i: (jnp.clip(i - FRAMES_IN, 0, FRAMES_IN - 1), 0, 0)),
            ),
            (held((FRAMES_OUT, SIDE, 384), bf16), step_spec((SIDE, 384))),
            (
                shaped(second.shape, bf16),
                pl.BlockSpec((8, 2 * STRIP, HID), lambda i: (0, i, 0)),
            ),
            (held((512, 1152), bf16), None),
        ],
        [
            pltpu.VMEM((FULL, 384), bf16),
            pltpu.VMEM((FULL, 128), f32),
            pltpu.VMEM((1152, 512), bf16),
            pltpu.VMEM((64 * GRID_ROWS, 512), f32),
            pltpu.VMEM((FULL, 384), bf16),
            pltpu.VMEM((FULL, 128), f32),
        ],
        cost(FRAMES_OUT, 56, 1),
        {7: 3},
        LONG,
    )


def join_hidden(got):
    out = call(
        join_kernel,
        "join_hidden",
        FRAMES_IN,
        [(got, pl.BlockSpec((8, 6 * STRIP, HID), lambda i: (0, i, 0)))],
        [
            (
                shaped((FRAMES_OUT, 2 * STRIP * 8, HID), bf16),
                pl.BlockSpec((3, 2 * STRIP * 8, HID), lambda i: (i, 0, 0)),
            )
        ],
        [],
        pl.CostEstimate(flops=0, bytes_accessed=1 << 21, transcendentals=0),
        memory=SMALL,
    )[0]
    out = out.reshape(FRAMES_OUT, STRIP * 8, 2, HID).transpose(0, 2, 1, 3)
    return out.reshape(1, FRAMES_OUT, 2, -1)


def tile_spec(cols, place):
    return pl.BlockSpec((cols * GRID_ROWS, HID), lambda i: (place(i), 0))


D_SHAPE = (512, STRIP * GRID_ROWS)


def turned(steps):
    return (
        pltpu.VMEM((512, steps * STRIP * GRID_ROWS), bf16),
        pl.BlockSpec(D_SHAPE, lambda i: (0, steps - 1 - i)),
    )


def backward_late(lim, weight, vec, saved, middle, og):
    own = STRIP * GRID_ROWS
    edge = held((2, EDGE_CELLS, 128), bf16)

    def first(i):
        return FRAMES_IN - 1 - jnp.minimum(i, FRAMES_IN - 1)

    def second(i):
        return jnp.minimum(2 * FRAMES_IN - 1 - i, FRAMES_IN - 1)

    return call(
        back_late_kernel,
        "fore_backward_late",
        2 * FRAMES_IN,
        [
            (lim, SMEM_SPEC),
            (weight, None),
            (vec, None),
            (saved, pl.BlockSpec((1, CELLS, 640), lambda i: (FRAMES_IN + first(i), 0, 0))),
            (og, tile_spec(KEPT, lambda i: 2 + first(i))),
            (middle, pl.BlockSpec((1, MID_CELLS, 640), lambda i: (second(i), 0, 0))),
            (og, tile_spec(MID_COLS, lambda i: MID_PLACE + second(i))),
        ],
        [
            turned(2 * FRAMES_IN),
            (held((56, 128), f32), None),
            (held((own, 128), f32), None),
            (held((own, 128), f32), None),
            (edge, None),
            (edge, None),
        ],
        [
            pltpu.VMEM((CELLS, 128), f32),
            pltpu.VMEM((CELLS, 128), f32),
            pltpu.VMEM((CELLS + 2 * GRID_ROWS, 512), bf16),
            pltpu.VMEM((CELLS, 128), f32),
            pltpu.VMEM((CELLS, 1152), f32),
        ],
        cost(2 * FRAMES_IN, 30, 1),
        memory=LONG,
    )


def backward_early(lim, weight, vec, saved, og, og_next, carried):
    return call(
        back_early_kernel,
        "fore_backward_early",
        FRAMES_IN,
        [
            (lim, SMEM_SPEC),
            (weight, None),
            (vec, None),
            (saved, step_spec((CELLS, 640), FRAMES_IN - 1)),
            (og, tile_spec(KEPT, lambda i: jnp.minimum(i, 1))),
            (og_next, tile_spec(KEPT, lambda i: jnp.maximum(i - 2, 0))),
            *[(array, None) for array in carried],
        ],
        [
            turned(FRAMES_IN),
            (held((56, 128), f32), None),
            (held((CELLS, 128), f32), None),
            (held((CELLS, 128), f32), None),
        ],
        [
            pltpu.VMEM((CELLS + 2 * GRID_ROWS, 512), bf16),
            pltpu.VMEM((CELLS, 128), f32),
            pltpu.VMEM((CELLS, 1152), f32),
        ],
        cost(FRAMES_IN, 36, 1),
        memory=MIDDLE,
    )


def backward_enc(lim, weight, weight_xb, vec, saved, dh, dc):
    last = FRAMES_IN - 1
    return call(
        enc_back_kernel,
        "enc_backward",
        FRAMES_IN,
        [
            (lim, SMEM_SPEC),
            (weight, None),
            (weight_xb, None),
            (vec, None),
            (saved, step_spec((ENC_CELLS, 640), last)),
            (dh, None),
            (dc, None),
        ],
        [
            turned(FRAMES_IN),
            (shaped((FRAMES_IN, GRID_ROWS, 256), f32), step_spec((GRID_ROWS, 256), last)),
            (shaped((56, 128), f32), None),
        ],
        [
            pltpu.VMEM((ENC_CELLS, 128), f32),
            pltpu.VMEM((ENC_CELLS, 128), f32),
            pltpu.VMEM((ENC_CELLS + 2 * GRID_ROWS, 512), bf16),
            pltpu.VMEM((ENC_CELLS, 128), f32),
            pltpu.VMEM((ENC_CELLS, 128), f32),
        ],
        cost(FRAMES_IN, 28, 1),
        memory=LONG,
    )


def sums_cost(frames):
    return pl.CostEstimate(
        flops=2 * frames * 256 * 512 * 1152, bytes_accessed=frames * 500000, transcendentals=0
    )


def gate_half(shape):
    return pl.BlockSpec((shape[0] // 2, shape[1]), lambda i: (i, 0))


def half_pair(shape, dtype):
    return (shaped(shape, dtype), gate_half(shape))


def late_sums(d_late, sides):
    return call(
        late_sums_kernel,
        "late_sums",
        2,
        [(d_late, gate_half(d_late.shape)), (sides, None)],
        [half_pair((512, 1152), f32)],
        [],
        sums_cost(2 * FRAMES_IN),
        memory=SMALL,
    )[0]


def early_sums(d_early, sides, g_late):
    return call(
        early_sums_kernel,
        "early_sums",
        2,
        [
            (d_early, gate_half(d_early.shape)),
            (sides, pl.BlockSpec((FRAMES_IN, SIDE, 384), lambda i: (0, 0, 0))),
            (g_late, gate_half(g_late.shape)),
        ],
        [half_pair((256, 1152), bf16), half_pair((256, 1152), bf16)],
        [],
        sums_cost(FRAMES_IN),
        memory=SMALL,
    )


def enc_sums(d_enc, sides, x_own, sums, fore_sums):
    move_f, _ = moves()
    return call(
        enc_sums_kernel,
        "enc_sums",
        2,
        [
            (d_enc, gate_half(d_enc.shape)),
            (sides, None),
            (x_own, None),
            (move_f, None),
            (sums, None),
            (fore_sums, None),
        ],
        [half_pair((256, 1408), bf16), half_pair((256, 1408), bf16)],
        [],
        sums_cost(FRAMES_IN),
        memory=SMALL,
    )


BAND = ("z", "core")


def column_tiles(got):
    return got.transpose(1, 0, 2, 3).reshape(-1, HID)


def passed(value, axis, steps):
    count = lax.axis_size(axis)
    return lax.ppermute(value, axis, [(k, (k + steps) % count) for k in range(count)])


def traded(blocks):
    chips = lax.axis_size("z")
    here, core = lax.axis_index("z"), lax.axis_index("core")
    pairs = blocks.reshape(chips, 2, *blocks.shape[1:])
    keep = lax.dynamic_index_in_dim(pairs, core, 1, keepdims=False)
    send = lax.dynamic_index_in_dim(pairs, 1 - core, 1, keepdims=False)
    other = passed(send, "core", 1)
    first = jnp.where(core == 0, keep, other)
    second = jnp.where(core == 0, other, keep)
    both = jnp.stack([first, second], axis=1)
    both = jnp.concatenate([both, both], axis=0)
    mine = lax.dynamic_slice_in_dim(both, here, chips)
    got = [mine[0]] + [passed(mine[s], "z", s) for s in range(1, chips)]
    order = jnp.stack(got[::-1] + got[::-1])
    ordered = lax.dynamic_slice_in_dim(order, chips - 1 - here, chips)
    return ordered.reshape(blocks.shape)


def grid_gather(share):
    count = lax.axis_size("grp")
    pieces = [share] + [passed(share, "grp", -s) for s in range(1, count)]
    place = lax.axis_index("grp")
    start = lax.rem(count - place, count) * share.shape[0]
    return lax.dynamic_slice_in_dim(jnp.concatenate(pieces + pieces), start, count * share.shape[0])


def chip_sum(keep, send):
    return (keep.astype(f32) + passed(send, "core", 1).astype(f32)).astype(bf16)


def slice_sum(total):
    chips = lax.axis_size("z") * lax.axis_size("grp")
    blocks = total.reshape(chips, -1, total.shape[1])
    got = lax.all_to_all(blocks, ("z", "grp"), 0, 0, tiled=True)
    return got


def arrived(got):
    return jnp.sum(got.astype(f32), axis=0)


def by_strips(
    frames,
    grid_size,
    out_grad,
    enc_hidden,
    enc_hidden_m,
    enc_hidden_v,
    fore_hidden,
    fore_hidden_m,
    fore_hidden_v,
    enc_input,
    enc_input_m,
    enc_input_v,
    cell_vectors,
    vectors_m,
    vectors_v,
):
    band = 2 * lax.axis_index("z") + lax.axis_index("core")
    part = cell_vectors.shape[0]
    pack = pack_parts(enc_hidden, enc_input, frames[0], cell_vectors.reshape(1, -1))
    pieces = [pack] + [passed(pack, "z", k) for k in range(1, 4)]
    cot = out_grad[0].reshape(FRAMES_OUT, 2, 8 * STRIP, HID).transpose(0, 2, 1, 3)
    first, second = cot_windows(cot)
    first, *pieces = lax.optimization_barrier((first, *pieces))
    mine = jnp.concatenate(pieces, axis=0)
    other = passed(mine, "core", 1)
    fore_part, mine = lax.optimization_barrier((fore_hidden.astype(bf16), mine))
    fore_pieces = [fore_part] + [passed(fore_part, "z", k) for k in range(1, 4)]
    enc_saved, enc_sides, x_own, h3, state, w_enc, weight_xb, vec = forward_enc(grid_size, mine, other)
    vec_enc, vec_fore = vec[:8], vec[8:]
    first, h3, *fore_pieces = lax.optimization_barrier((first, h3, *fore_pieces))
    fore_mine = jnp.concatenate(fore_pieces, axis=0)
    fore_other = passed(fore_mine, "core", 1)
    first_got = lax.all_to_all(first, BAND, 0, 0, tiled=True)
    fore_saved, fore_middle, fore_sides, second, w_fore = forward_fore(
        grid_size, fore_mine, fore_other, vec_fore, h3, state, second
    )
    second_got = lax.all_to_all(second, BAND, 0, 0, tiled=True)
    og = column_tiles(first_got)
    d_late, sums, dh, dc, left, right = backward_late(
        grid_size, w_fore, vec_fore, fore_saved, fore_middle, og
    )
    from_left = from_behind(right, BAND, 1)
    from_right = from_behind(left, BAND, -1)
    g_late = late_sums(d_late, fore_sides)
    second_got, from_right = lax.optimization_barrier((second_got, from_right))
    og_next = second_got.reshape(8, SECOND_COLS, 2, HID)[:, SECOND_PLACE:]
    d_early, sums, dh, dc = backward_early(
        grid_size,
        w_fore,
        vec_fore,
        fore_saved,
        og,
        column_tiles(og_next),
        (sums, dh, dc, from_left, from_right),
    )
    fore_total = chip_sum(*early_sums(d_early, fore_sides, g_late))
    fore_total, dh = lax.optimization_barrier((fore_total, dh))
    fore_got = slice_sum(fore_total)
    d_enc, dx, enc_sums_of = backward_enc(grid_size, w_enc, weight_xb, vec_enc, enc_saved, dh, dc)
    keep, send = enc_sums(d_enc, enc_sides, x_own, enc_sums_of, sums)
    fore_got, keep, send, dx, second_got = lax.optimization_barrier((fore_got, keep, send, dx, second_got))
    enc_sum = chip_sum(keep, send)
    enc_sum, second_got, dx, fore_got = lax.optimization_barrier((enc_sum, second_got, dx, fore_got))
    enc_got = slice_sum(enc_sum)
    input_got = traded(dx.reshape(FRAMES_IN, 8, 2, 256).transpose(1, 0, 2, 3))
    fore_sum = arrived(fore_got)
    enc_total = arrived(enc_got)
    tail = grid_gather(jnp.concatenate([enc_total, fore_sum], axis=1).astype(bf16)).astype(f32)
    enc_share = tail[:, :1152]
    input_share = tail[:, 1152:1296]
    fore_share = tail[:, 1408:]
    vector_share = lax.dynamic_slice_in_dim(enc_total[:, 1296:1408].reshape(-1), band * part, part)
    return (
        join_hidden(second_got),
        input_got.transpose(1, 2, 0, 3).reshape(1, FRAMES_IN, 2, -1),
        *adam_update(enc_hidden, enc_hidden_m, enc_hidden_v, enc_share, matrix_rate),
        *adam_update(fore_hidden, fore_hidden_m, fore_hidden_v, fore_share, matrix_rate),
        *adam_update(enc_input, enc_input_m, enc_input_v, input_share, matrix_rate),
        *adam_update(cell_vectors, vectors_m, vectors_v, vector_share, vector_rate),
    )


def solution(mesh):
    groups, bands = mesh.shape["grp"], mesh.shape["band"]

    def run(frames, grid_size, out_grad, *rest):
        strips = frames.shape[2] == GRID_ROWS and out_grad.shape[3] == STRIP * bands * HID
        strips = strips and bands == 8 and groups == 4
        if strips:
            places = Mesh(mesh.devices.reshape(groups, bands // 2, 2), ("grp", *BAND))
            body, band = by_strips, BAND
        else:
            places, body, band = mesh, by_rows, "band"
        grid = P("grp", None, band, None)
        matrix = P(band, None)
        vector = P(band)
        return jax.shard_map(
            body,
            mesh=places,
            in_specs=(grid, P("grp", None), grid, *[matrix] * 9, *[vector] * 3),
            out_specs=(grid, grid, *[matrix] * 12, *[vector] * 4),
            check_vma=False,
        )(frames, grid_size, out_grad, *rest)

    return run
```
